512 devices in a mesh: dom: 64 (over x, z), sub: 8 (over y, core).
Axes of the slice: x: 4, y: 4, z: 16, core: 2. Of those that a mesh axis runs over, the one named last changes fastest.
Arguments:
- rhs: float32 [204800], P(('dom', 'sub')), may hold values from -6 to 6
- diag_blocks: bfloat16 [2048, 10000], P(('dom', 'sub'))
- face_blocks: bfloat16 [2048, 40000], P(('dom', 'sub')), may hold values from -0.21875 to 0.21875
- precond_blocks: bfloat16 [2048, 10000], P(('dom', 'sub'))
- neighbours: int32 [2048, 4], P(('dom', 'sub')), may hold values from -1 to 2047, as said below
Outputs:
- adjoint: float32 [204800], P(('dom', 'sub'))
The draws below stay inside these ranges and needn't reach their ends.
Inputs may be any that keep to these rules, and one draw needn't show every extreme that they name: `neighbours`: let element g lie on device d * 8 + s (slab d, position s), g = (d * 8 + s) * 4 + i. Face 1 names an element of device (d + 1, s) or -1; face 0 names one of device (d - 1, s) or -1; faces 2 and 3 name elements of slab d (any position, itself possible). Element e's face 1 names m exactly when m's face 0 names e, and e's face 2 names m exactly when m's face 3 names e. Face 0 is -1 in slab 0, face 1 in the last slab.
All inputs are finite; a program needn't handle non-finite values.
Results may differ from the reference program's by a relative error of at most 0.003.
Values sent between devices are 32-bit elements; how exact they have to be, the bound alone decides.
A program may use at most 64 MiB of HBM per device.

```python
import math
import jax
import jax.numpy as jnp
from jax import lax

B = 100
E_DEV = 4
NE = 2048
N_DOM = 64
N_SUB = 8


def near_identity(key, low_scale, high_scale, spread):
    count = E_DEV * N_DOM * N_SUB
    scale_key, noise_key = jax.random.split(key)
    scales = jnp.exp(jax.random.uniform(scale_key, (count, 1, 1), jnp.float32, math.log(low_scale), math.log(high_scale)))
    noise = jax.random.normal(noise_key, (count, B, B), jnp.float32)
    blocks = scales * (jnp.eye(B, dtype=jnp.float32)[None] + noise * (spread / math.sqrt(B)))
    return blocks.reshape(count, B * B).astype(jnp.bfloat16)


def draw_diag_blocks(key, part):
    key = jax.random.fold_in(key, 21)
    return near_identity(key, 1.0, 4.0, 0.5)


def draw_precond_blocks(key, part):
    key = jax.random.fold_in(key, 31)
    return near_identity(key, 0.25, 1.0, 0.3)


def draw_neighbours(key, part):
    key = jax.random.fold_in(key, 41)
    slab = E_DEV * N_SUB
    cross_keys = jax.random.split(jax.random.fold_in(key, 1), N_DOM * N_SUB)
    upper = jax.vmap(lambda k: jax.random.permutation(k, E_DEV))(cross_keys).reshape(N_DOM, N_SUB, E_DEV)
    lower = jnp.argsort(upper, axis=-1, stable=True).astype(jnp.int32)
    opened = jax.random.randint(jax.random.fold_in(key, 2), (N_DOM, N_SUB, E_DEV), 0, 4) > 0
    slab_index = jnp.arange(N_DOM, dtype=jnp.int32)[:, None, None]
    sub_index = jnp.arange(N_SUB, dtype=jnp.int32)[None, :, None]
    face_one = jnp.where(opened & (slab_index < N_DOM - 1), ((slab_index + 1) * N_SUB + sub_index) * E_DEV + upper, -1)
    lower_shift = jnp.concatenate([jnp.zeros_like(lower[:1]), lower[:-1]], axis=0)
    opened_shift = jnp.concatenate([jnp.zeros_like(opened[:1]), opened[:-1]], axis=0)
    opened_down = jnp.take_along_axis(opened_shift, lower_shift, axis=-1)
    face_zero = jnp.where(opened_down & (slab_index > 0), ((slab_index - 1) * N_SUB + sub_index) * E_DEV + lower_shift, -1)
    inner_keys = jax.random.split(jax.random.fold_in(key, 3), N_DOM)
    forward = jax.vmap(lambda k: jax.random.permutation(k, slab))(inner_keys).astype(jnp.int32)
    backward = jnp.argsort(forward, axis=-1, stable=True).astype(jnp.int32)
    base = jnp.arange(N_DOM, dtype=jnp.int32)[:, None] * slab
    face_two = base + forward
    face_three = base + backward
    return jnp.stack([face_zero.reshape(-1), face_one.reshape(-1), face_two.reshape(-1), face_three.reshape(-1)], axis=1).astype(jnp.int32)


def steps_of(own_key, shape, cuts, least, top_value):
    def one(position, parts):
        heights = jax.random.uniform(jax.random.fold_in(jax.random.fold_in(own_key, 6), position), (parts,), jnp.float32, least / len(cuts), top_value / len(cuts))
        return jnp.repeat(jnp.exp(heights), shape[position] // parts).reshape((-1,) + (1,) * (len(shape) - position - 1))

    factor_of = one(*cuts[0])
    for cut in cuts[1:]:
        factor_of = factor_of * one(*cut)
    return factor_of


def scatter_about(stream_key, shape, width, most, cuts=(), kind=jnp.bfloat16):
    level = steps_of(stream_key, shape, cuts, -0.22, 0.18) if cuts else 1.0
    array = jax.random.normal(stream_key, shape, jnp.float32) * width * level
    return jnp.minimum(jnp.maximum(array, -most), most).astype(kind)


def setup_inputs(seed: int = 0) -> dict:
    seeds = jax.random.split(jax.random.key(seed), 6)
    return {
        "rhs": scatter_about(seeds[0], (NE * B,), 1.0, 6.0, ((0, 512),), jnp.float32),
        "diag_blocks": draw_diag_blocks(jax.random.fold_in(seeds[5], 71), 0),
        "face_blocks": scatter_about(seeds[2], (NE, 4 * B * B), (8 * B) ** -0.5, 0.21875, ((0, 512),)),
        "precond_blocks": draw_precond_blocks(jax.random.fold_in(seeds[5], 71), 0),
        "neighbours": draw_neighbours(jax.random.fold_in(seeds[5], 71), 0),
    }


def slab_products(vector, diag_blocks, face_blocks):
    low = vector.reshape(N_DOM, -1, B).astype(jnp.bfloat16)

    def one_slab(items):
        diag, faces, part = items
        part = part.astype(jnp.float32)
        diag = diag.reshape(-1, B, B).astype(jnp.float32)
        faces = faces.reshape(-1, 4, B, B).astype(jnp.float32)
        own = jnp.einsum('eab,ea->eb', diag, part, precision=lax.Precision.HIGHEST)
        sent = jnp.einsum('ekab,ea->ekb', faces, part, precision=lax.Precision.HIGHEST)
        return (own, sent)
    return lax.map(one_slab, (diag_blocks.reshape(N_DOM, -1, B * B), face_blocks.reshape(N_DOM, -1, 4 * B * B), low))

def apply_operator(vector, diag_blocks, face_blocks, neighbours):
    count = neighbours.shape[0]
    own, sent = slab_products(vector, diag_blocks, face_blocks)
    own = own.reshape(count, B)
    sent = sent.reshape(count * 4, B)
    target = jnp.where(neighbours < 0, count, neighbours).reshape(-1).astype(jnp.int32)
    image = own.at[target].add(sent, mode='drop')
    return image.reshape(-1)

def precondition(vector, precond_blocks):
    low = vector.reshape(N_DOM, -1, B).astype(jnp.bfloat16)

    def one_slab(items):
        blocks, part = items
        blocks = blocks.reshape(-1, B, B).astype(jnp.float32)
        return jnp.einsum('eab,eb->ea', blocks, part.astype(jnp.float32), precision=lax.Precision.HIGHEST)
    return lax.map(one_slab, (precond_blocks.reshape(N_DOM, -1, B * B), low)).reshape(-1)

def givens_solve(beta, h11, h21, h12, h22, h32):
    first_r = jnp.sqrt(h11 * h11 + h21 * h21)
    cosine = h11 / first_r
    sine = h21 / first_r
    upper = cosine * h12 + sine * h22
    lower = cosine * h22 - sine * h12
    second_r = jnp.sqrt(lower * lower + h32 * h32)
    second_y = lower / second_r * (-sine * beta) / second_r
    first_y = (cosine * beta - upper * second_y) / first_r
    return (first_y, second_y)

def reference(rhs, diag_blocks, face_blocks, precond_blocks, neighbours):
    beta = jnp.sqrt(jnp.sum(rhs * rhs))
    basis_one = rhs / beta
    search_one = precondition(basis_one, precond_blocks)
    work = apply_operator(search_one, diag_blocks, face_blocks, neighbours)
    h11 = jnp.sum(work * basis_one)
    work = work - h11 * basis_one
    h21 = jnp.sqrt(jnp.sum(work * work))
    basis_two = work / h21
    search_two = precondition(basis_two, precond_blocks)
    work = apply_operator(search_two, diag_blocks, face_blocks, neighbours)
    h12 = jnp.sum(work * basis_one)
    work = work - h12 * basis_one
    h22 = jnp.sum(work * basis_two)
    work = work - h22 * basis_two
    h32 = jnp.sqrt(jnp.sum(work * work))
    first_y, second_y = givens_solve(beta, h11, h21, h12, h22, h32)
    return first_y * search_one + second_y * search_two
```

```python
import functools

import jax
import jax.numpy as jnp
from jax import lax
from jax.experimental import pallas as pl
from jax.experimental.pallas import tpu as pltpu
from jax.sharding import PartitionSpec as P

B = 100
E = 4
LANES = 128
TILES = 25
CHIPS_X = 4
SCALES = (2.0**-44, 1.0, 2.0**44)
SHRINK = 2.0**-12
MESH = pl.DeviceIdType.MESH
F32 = jnp.float32


def lane_of(rows=E):
    return lax.broadcasted_iota(jnp.int32, (rows, LANES), 1)


def periodic(vector):
    lane = lane_of()
    base = jnp.where(lane < B, vector, pltpu.roll(vector, B, 1))
    tiles = []
    for j in range(TILES):
        offset = 28 * j % B
        if offset == 0:
            tiles.append(base)
        else:
            left = pltpu.roll(base, LANES - offset, 1)
            right = pltpu.roll(base, B - offset, 1)
            tiles.append(jnp.where(lane < LANES - offset, left, right))
    return tiles


def tile_at(ref, j):
    width = min(LANES, ref.shape[1] - j * LANES)
    part = ref[:, j * LANES : j * LANES + width].astype(F32)
    if width < LANES:
        part = jnp.concatenate([part, jnp.zeros((E, LANES - width), F32)], axis=1)
    return part


def row_products(ref, vector):
    lane = lane_of()
    tiles = periodic(vector)
    count = -(-B * B // LANES)
    products = [tile_at(ref, j) * tiles[j % TILES] for j in range(count)]
    sums = []
    for a in range(B):
        j, start = divmod(B * a, LANES)
        if start + B <= LANES:
            row = products[j]
            if start > 0:
                row = jnp.where(lane >= start, row, 0.0)
            if start + B < LANES:
                row = jnp.where(lane < start + B, row, 0.0)
        else:
            row = jnp.where(lane >= start, products[j], jnp.where(lane < start + B - LANES, products[j + 1], 0.0))
        sums.append(jnp.sum(row, axis=1, keepdims=True))
    return sums


def fold(tiles):
    lane = lane_of()
    flat = jnp.concatenate(tiles, axis=1)
    width = TILES * LANES
    while width > B:
        width //= 2
        flat = flat[:, :width] + flat[:, width : 2 * width]
    return jnp.concatenate([flat, jnp.zeros((E, LANES - B), F32)], axis=1)


def column_products(ref, first_row, values):
    lane = lane_of()
    start, stop = first_row * B, (first_row + B) * B
    sums = [None] * TILES
    wide = [jnp.broadcast_to(value, (E, LANES)) for value in values]
    for j in range(start // LANES, -(-stop // LANES)):
        factor = None
        for row in range(j * LANES // B, (j * LANES + LANES - 1) // B + 1):
            begin = row * B - j * LANES
            inside = first_row <= row < first_row + B
            value = wide[row - first_row] if inside else jnp.zeros((E, LANES), F32)
            factor = value if factor is None else jnp.where(lane >= begin, value, factor)
        term = tile_at(ref, j) * factor
        slot = j % TILES
        sums[slot] = term if sums[slot] is None else sums[slot] + term
    return fold(sums)


def as_rows(values):
    lane = lane_of()
    out = jnp.zeros((E, LANES), F32)
    for a, value in enumerate(values):
        out = jnp.where(lane == a, value, out)
    return out


def kernel(
    sizes, rhs_hbm, diag_hbm, face_hbm, prec_hbm, near_ref, out_ref,
    rhs_ref, diag_ref, face_ref, prec_ref, load_sem,
    out_box, in_box, plane_box, column_box, plane_out, column_out,
    send_sem, recv_sem, plane_sem, column_sem,
):
    doms, subs = sizes
    chips_z = doms // CHIPS_X
    d, s = lax.axis_index("dom"), lax.axis_index("sub")
    x, z = d // chips_z, d % chips_z
    plane, slab = CHIPS_X * subs, subs * E

    loads = [
        pltpu.make_async_copy(src, dst, load_sem.at[i])
        for i, (src, dst) in enumerate(
            [(rhs_hbm, rhs_ref), (prec_hbm, prec_ref), (diag_hbm, diag_ref), (face_hbm, face_ref)]
        )
    ]
    for load in loads:
        load.start()

    def plane_mate(k):
        return ((x + k // subs) % CHIPS_X) * chips_z + z, (s + k % subs) % subs

    def column_mate(k):
        return x * chips_z + (z + k) % chips_z, s

    above, below = (d + 1) % doms, (d + doms - 1) % doms
    barrier = pltpu.get_barrier_semaphore()

    def greet(device):
        pl.semaphore_signal(barrier, inc=1, device_id=device, device_id_type=MESH)

    greet((above, s))
    greet((below, s))

    @pl.loop(1, plane)
    def _(k):
        greet(plane_mate(k))

    @pl.loop(1, chips_z)
    def _(k):
        greet(column_mate(k))

    goal = {}
    for e in range(E):
        for face in range(4):
            near = near_ref[e, face]
            if face >= 2:
                row = (near - d * slab - s * E + slab) % slab
            else:
                row = near % E + slab + (E if face == 0 else 0)
            goal[e, face] = jnp.where(near >= 0, row, -1)

    def apply(vector, step):
        if step == 0:
            loads[1].wait()
        values = row_products(prec_ref, vector)
        if step == 0:
            loads[3].wait()
        sent = [column_products(face_ref, face * B, values) for face in range(4)]
        row = lax.broadcasted_iota(jnp.int32, (slab, LANES), 0)
        inner = jnp.zeros((slab, LANES), F32)
        for face in (2, 3):
            for e in range(E):
                inner = inner + jnp.where(row == goal[e, face], sent[face][e : e + 1], 0.0)
        row = lax.broadcasted_iota(jnp.int32, (2 * E, LANES), 0) + slab
        outer = jnp.zeros((2 * E, LANES), F32)
        for face in (0, 1):
            for e in range(E):
                outer = outer + jnp.where(row == goal[e, face], sent[face][e : e + 1], 0.0)
        for k in range(1, subs):
            out_box[step, k - 1] = inner[E * k : E * k + E]
        out_box[step, subs - 1] = outer[:E]
        out_box[step, subs] = outer[E:]
        if step == 0:
            pl.semaphore_wait(barrier, plane - 1 + chips_z - 1 + 2)
        for k in range(subs + 1):
            if k < subs - 1:
                device = (d, (s + k + 1) % subs)
            else:
                device = (above if k == subs - 1 else below, s)
            pltpu.make_async_remote_copy(
                src_ref=out_box.at[step, k],
                dst_ref=in_box.at[step, k],
                send_sem=send_sem.at[step],
                recv_sem=recv_sem.at[step],
                device_id=device,
                device_id_type=MESH,
            ).start()
        if step == 0:
            loads[2].wait()
        image = inner[:E] + column_products(diag_ref, 0, values)
        search = as_rows(values)
        pltpu.make_async_copy(in_box.at[step], in_box.at[step], recv_sem.at[step]).wait()
        for k in range(subs + 1):
            image = image + in_box[step, k]
        return search, image

    loads[0].wait()
    flat = jnp.concatenate([rhs_ref[...] * SHRINK, jnp.zeros((1, E * LANES - E * B), F32)], axis=1)
    start = jnp.concatenate([flat[:, B * e : B * e + B] for e in range(E)], axis=0)
    start = jnp.concatenate([start, jnp.zeros((E, LANES - B), F32)], axis=1)
    search_one, image_one = apply(start, 0)
    search_two, image_two = apply(image_one, 1)

    products = [image_one * start, image_two * start]
    for scale in SCALES:
        one, two = image_one * scale, image_two * (scale * scale)
        products += [one * one, one * two, two * two]
    lane = lane_of(1)
    message = jnp.zeros((1, LANES), F32)
    for q, product in enumerate(products):
        total = jnp.sum(jnp.sum(product, axis=0, keepdims=True), axis=1, keepdims=True)
        message = jnp.where(lane == q, total, message)

    def share(message, mate, count, box, out, sems):
        out[...] = message

        @pl.loop(1, count)
        def _(k):
            pltpu.make_async_remote_copy(
                src_ref=out,
                dst_ref=box.at[pl.ds(k, 1)],
                send_sem=sems.at[0],
                recv_sem=sems.at[1],
                device_id=mate(k),
                device_id_type=MESH,
            ).start()

        box[0:1] = message
        arrived = box.at[pl.ds(1, count - 1)]
        pltpu.make_async_copy(arrived, arrived, sems.at[1]).wait()
        return jnp.sum(box[...], axis=0, keepdims=True)

    message = share(message, plane_mate, plane, plane_box, plane_out, plane_sem)
    message = share(message, column_mate, chips_z, column_box, column_out, column_sem)

    def entry(q):
        return jnp.sum(jnp.where(lane == q, message, 0.0), axis=1, keepdims=True)

    def pick(q):
        low, mid, high = (entry(2 + 3 * i + q) for i in range(3))
        return jnp.where(too_large, low, jnp.where(too_small, high, mid))

    size = entry(2 + 3 + 2)
    too_large = jnp.logical_not(size < 1e26)
    too_small = size < 1e-26
    scale = jnp.where(too_large, SCALES[0], jnp.where(too_small, SCALES[2], SCALES[1]))
    one_one, one_two, two_two = pick(0), pick(1), pick(2)
    one_rhs, two_rhs = entry(0) * scale, entry(1) * scale * scale
    slope = one_two / one_one
    rest = jnp.maximum(two_two - slope * one_two, two_two * 2.0**-22)
    second = (two_rhs - slope * one_rhs) / rest
    first = one_rhs / one_one - slope * second
    answer = first * scale * (search_one * (1.0 / SHRINK)) + second * scale * scale * (search_two * (1.0 / SHRINK))
    out_ref[...] = jnp.concatenate([answer[e : e + 1, :B] for e in range(E)], axis=1)

    for step in range(2):
        pltpu.make_async_copy(out_box.at[step], out_box.at[step], send_sem.at[step]).wait()
    for box, count, sems in ((plane_box, plane, plane_sem), (column_box, chips_z, column_sem)):
        sent = box.at[pl.ds(1, count - 1)]
        pltpu.make_async_copy(sent, sent, sems.at[0]).wait()


def solution(mesh):
    doms, subs = mesh.shape["dom"], mesh.shape["sub"]
    chips_z = doms // CHIPS_X

    def body(rhs, diag, faces, precond, neighbours):
        out = pl.pallas_call(
            functools.partial(kernel, (doms, subs)),
            out_shape=jax.ShapeDtypeStruct((1, E * B), F32),
            in_specs=[pl.BlockSpec(memory_space=pltpu.HBM)] * 4 + [pl.BlockSpec(memory_space=pltpu.SMEM)],
            out_specs=pl.BlockSpec(memory_space=pltpu.VMEM),
            scratch_shapes=[
                pltpu.VMEM((1, E * B), F32),
                pltpu.VMEM(diag.shape, diag.dtype),
                pltpu.VMEM(faces.shape, faces.dtype),
                pltpu.VMEM(precond.shape, precond.dtype),
                pltpu.SemaphoreType.DMA((4,)),
                pltpu.VMEM((2, subs + 1, E, LANES), F32),
                pltpu.VMEM((2, subs + 1, E, LANES), F32),
                pltpu.VMEM((CHIPS_X * subs, LANES), F32),
                pltpu.VMEM((chips_z, LANES), F32),
                pltpu.VMEM((1, LANES), F32),
                pltpu.VMEM((1, LANES), F32),
                pltpu.SemaphoreType.DMA((2,)),
                pltpu.SemaphoreType.DMA((2,)),
                pltpu.SemaphoreType.DMA((2,)),
                pltpu.SemaphoreType.DMA((2,)),
            ],
            compiler_params=pltpu.CompilerParams(
                collective_id=0, has_side_effects=True, vmem_limit_bytes=32 * 2**20
            ),
            cost_estimate=pl.CostEstimate(flops=2_000_000, bytes_accessed=500_000, transcendentals=0),
        )(rhs.reshape(1, -1), diag, faces, precond, neighbours)
        return out.reshape(-1)

    rows = P(("dom", "sub"), None)
    flat = P(("dom", "sub"))
    return jax.shard_map(
        body, mesh=mesh, in_specs=(flat, rows, rows, rows, rows), out_specs=flat, check_vma=False
    )
```

```python
import functools

import jax
import jax.numpy as jnp
from jax import lax
from jax.experimental import pallas as pl
from jax.experimental.pallas import tpu as pltpu
from jax.sharding import PartitionSpec as P

B = 100
E = 4
LANES = 128
TILES = 25
CHIPS_X = 4
SCALES = (2.0**-44, 1.0, 2.0**44)
SHRINK = 2.0**-12
MESH = pl.DeviceIdType.MESH
F32 = jnp.float32


def lane_of(rows=E):
    return lax.broadcasted_iota(jnp.int32, (rows, LANES), 1)


def periodic(vector):
    lane = lane_of()
    base = jnp.where(lane < B, vector, pltpu.roll(vector, B, 1))
    tiles = []
    for j in range(TILES):
        offset = 28 * j % B
        if offset == 0:
            tiles.append(base)
        else:
            left = pltpu.roll(base, LANES - offset, 1)
            right = pltpu.roll(base, B - offset, 1)
            tiles.append(jnp.where(lane < LANES - offset, left, right))
    return tiles


def tile_at(ref, j):
    width = min(LANES, ref.shape[1] - j * LANES)
    part = ref[:, j * LANES : j * LANES + width].astype(F32)
    if width < LANES:
        part = jnp.concatenate([part, jnp.zeros((E, LANES - width), F32)], axis=1)
    return part


def row_products(ref, vector):
    lane = lane_of()
    tiles = periodic(vector)
    count = -(-B * B // LANES)
    products = [tile_at(ref, j) * tiles[j % TILES] for j in range(count)]
    sums = []
    for a in range(B):
        j, start = divmod(B * a, LANES)
        if start + B <= LANES:
            row = products[j]
            if start > 0:
                row = jnp.where(lane >= start, row, 0.0)
            if start + B < LANES:
                row = jnp.where(lane < start + B, row, 0.0)
        else:
            row = jnp.where(lane >= start, products[j], jnp.where(lane < start + B - LANES, products[j + 1], 0.0))
        sums.append(jnp.sum(row, axis=1, keepdims=True))
    return sums


def fold(tiles):
    lane = lane_of()
    flat = jnp.concatenate(tiles, axis=1)
    width = TILES * LANES
    while width > B:
        width //= 2
        flat = flat[:, :width] + flat[:, width : 2 * width]
    return jnp.concatenate([flat, jnp.zeros((E, LANES - B), F32)], axis=1)


def column_products(ref, first_row, values):
    lane = lane_of()
    start, stop = first_row * B, (first_row + B) * B
    sums = [None] * TILES
    wide = [jnp.broadcast_to(value, (E, LANES)) for value in values]
    for j in range(start // LANES, -(-stop // LANES)):
        factor = None
        for row in range(j * LANES // B, (j * LANES + LANES - 1) // B + 1):
            begin = row * B - j * LANES
            inside = first_row <= row < first_row + B
            value = wide[row - first_row] if inside else jnp.zeros((E, LANES), F32)
            factor = value if factor is None else jnp.where(lane >= begin, value, factor)
        term = tile_at(ref, j) * factor
        slot = j % TILES
        sums[slot] = term if sums[slot] is None else sums[slot] + term
    return fold(sums)


def as_rows(values):
    lane = lane_of()
    out = jnp.zeros((E, LANES), F32)
    for a, value in enumerate(values):
        out = jnp.where(lane == a, value, out)
    return out


def kernel(
    sizes, rhs_hbm, diag_hbm, face_hbm, prec_hbm, near_hbm, out_ref,
    rhs_ref, diag_ref, face_ref, prec_ref, near_ref, load_sem,
    out_box, in_box, plane_box, column_box, plane_out, column_out,
    send_sem, recv_sem, plane_sem, column_sem, known_a, known_b, known_c,
):
    doms, subs = sizes
    chips_z = doms // CHIPS_X
    d, s = lax.axis_index("dom"), lax.axis_index("sub")
    x, z = d // chips_z, d % chips_z
    plane, slab = CHIPS_X * subs, subs * E

    loads = [
        pltpu.make_async_copy(src, dst, load_sem.at[i])
        for i, (src, dst) in enumerate(
            [
                (rhs_hbm, rhs_ref), (prec_hbm, prec_ref), (face_hbm, face_ref), (near_hbm, near_ref),
                (diag_hbm, diag_ref),
            ]
        )
    ]
    for load in loads:
        load.start()

    def plane_mate(k):
        return ((x + k // subs) % CHIPS_X) * chips_z + z, (s + k % subs) % subs

    def column_mate(k):
        return x * chips_z + (z + k) % chips_z, s

    above, below = (d + 1) % doms, (d + doms - 1) % doms
    barrier = pltpu.get_barrier_semaphore()

    def tell(semaphore, device):
        pl.semaphore_signal(semaphore, inc=1, device_id=device, device_id_type=MESH)

    def along_z(step):
        return x * chips_z + (z + step + chips_z) % chips_z, s

    def along_x(step):
        return (x + step + CHIPS_X) % CHIPS_X * chips_z + z, s

    def greet():
        for k in range(1, subs):
            tell(barrier, (d, (s + k) % subs))
        for device in ((above, s), (below, s), along_z(1), along_z(-1), along_x(1), along_x(-1)):
            tell(barrier, device)

    greeted = subs - 1 + 6

    def tell_a():
        for device in (along_z(1), along_z(-1), along_x(1), along_x(-1)):
            tell(known_a, device)

    def tell_b():
        pl.semaphore_wait(known_a, 4)
        for device in (along_z(2), along_z(-2), along_x(1)):
            tell(known_b, device)

    def tell_c():
        pl.semaphore_wait(known_b, 3)
        for device in (along_z(4), along_z(-4)):
            tell(known_c, device)

    greet()

    def apply(vector, step):
        if step == 0:
            loads[1].wait()
        values = row_products(prec_ref, vector)
        if step == 0:
            loads[2].wait()
        sent = [column_products(face_ref, face * B, values) for face in range(4)]
        row = lax.broadcasted_iota(jnp.int32, (slab, LANES), 0)
        inner = jnp.zeros((slab, LANES), F32)
        for face in (2, 3):
            for e in range(E):
                inner = inner + jnp.where(row == goal[e, face], sent[face][e : e + 1], 0.0)
        row = lax.broadcasted_iota(jnp.int32, (2 * E, LANES), 0) + slab
        outer = jnp.zeros((2 * E, LANES), F32)
        for face in (0, 1):
            for e in range(E):
                outer = outer + jnp.where(row == goal[e, face], sent[face][e : e + 1], 0.0)
        for k in range(1, subs):
            out_box[step, k - 1] = inner[E * k : E * k + E]
        out_box[step, subs - 1] = outer[:E]
        out_box[step, subs] = outer[E:]
        if step == 0:
            pl.semaphore_wait(barrier, greeted)
        for k in range(subs + 1):
            if k < subs - 1:
                device = (d, (s + k + 1) % subs)
            else:
                device = (above if k == subs - 1 else below, s)
            pltpu.make_async_remote_copy(
                src_ref=out_box.at[step, k],
                dst_ref=in_box.at[step, k],
                send_sem=send_sem.at[step],
                recv_sem=recv_sem.at[step],
                device_id=device,
                device_id_type=MESH,
            ).start()
        if step == 0:
            tell_a()
            loads[4].wait()
        image = inner[:E] + column_products(diag_ref, 0, values)
        search = as_rows(values)
        tell_b() if step == 0 else tell_c()
        pltpu.make_async_copy(in_box.at[step], in_box.at[step], recv_sem.at[step]).wait()
        for k in range(subs + 1):
            image = image + in_box[step, k]
        return search, image

    loads[3].wait()
    goal = {}
    for e in range(E):
        for face in range(4):
            near = near_ref[e, face]
            if face >= 2:
                row = (near - d * slab - s * E + slab) % slab
            else:
                row = near % E + slab + (E if face == 0 else 0)
            goal[e, face] = jnp.where(near >= 0, row, -1)

    loads[0].wait()
    flat = jnp.concatenate([rhs_ref[...] * SHRINK, jnp.zeros((1, E * LANES - E * B), F32)], axis=1)
    start = jnp.concatenate([flat[:, B * e : B * e + B] for e in range(E)], axis=0)
    start = jnp.concatenate([start, jnp.zeros((E, LANES - B), F32)], axis=1)
    search_one, image_one = apply(start, 0)
    search_two, image_two = apply(image_one, 1)

    products = [image_one * start, image_two * start]
    for scale in SCALES:
        one, two = image_one * scale, image_two * (scale * scale)
        products += [one * one, one * two, two * two]
    lane = lane_of(1)
    message = jnp.zeros((1, LANES), F32)
    for q, product in enumerate(products):
        total = jnp.sum(jnp.sum(product, axis=0, keepdims=True), axis=1, keepdims=True)
        message = jnp.where(lane == q, total, message)

    def share(message, mate, count, box, out, sems):
        out[...] = message

        @pl.loop(1, count)
        def _(k):
            pltpu.make_async_remote_copy(
                src_ref=out,
                dst_ref=box.at[pl.ds(k, 1)],
                send_sem=sems.at[0],
                recv_sem=sems.at[1],
                device_id=mate(k),
                device_id_type=MESH,
            ).start()

        box[0:1] = message
        arrived = box.at[pl.ds(1, count - 1)]
        pltpu.make_async_copy(arrived, arrived, sems.at[1]).wait()
        return jnp.sum(box[...], axis=0, keepdims=True)

    message = share(message, plane_mate, plane, plane_box, plane_out, plane_sem)
    pl.semaphore_wait(known_c, 2)
    message = share(message, column_mate, chips_z, column_box, column_out, column_sem)

    def entry(q):
        return jnp.sum(jnp.where(lane == q, message, 0.0), axis=1, keepdims=True)

    def pick(q):
        low, mid, high = (entry(2 + 3 * i + q) for i in range(3))
        return jnp.where(too_large, low, jnp.where(too_small, high, mid))

    size = entry(2 + 3 + 2)
    too_large = jnp.logical_not(size < 1e26)
    too_small = size < 1e-26
    scale = jnp.where(too_large, SCALES[0], jnp.where(too_small, SCALES[2], SCALES[1]))
    one_one, one_two, two_two = pick(0), pick(1), pick(2)
    one_rhs, two_rhs = entry(0) * scale, entry(1) * scale * scale
    slope = one_two / one_one
    rest = jnp.maximum(two_two - slope * one_two, two_two * 2.0**-22)
    second = (two_rhs - slope * one_rhs) / rest
    first = one_rhs / one_one - slope * second
    answer = first * scale * (search_one * (1.0 / SHRINK)) + second * scale * scale * (search_two * (1.0 / SHRINK))
    out_ref[...] = jnp.concatenate([answer[e : e + 1, :B] for e in range(E)], axis=1)

    for step in range(2):
        pltpu.make_async_copy(out_box.at[step], out_box.at[step], send_sem.at[step]).wait()
    for box, count, sems in ((plane_box, plane, plane_sem), (column_box, chips_z, column_sem)):
        sent = box.at[pl.ds(1, count - 1)]
        pltpu.make_async_copy(sent, sent, sems.at[0]).wait()


def solution(mesh):
    doms, subs = mesh.shape["dom"], mesh.shape["sub"]
    chips_z = doms // CHIPS_X

    def body(rhs, diag, faces, precond, neighbours):
        out = pl.pallas_call(
            functools.partial(kernel, (doms, subs)),
            out_shape=pltpu.VMEM((1, E * B), F32),
            in_specs=[pl.BlockSpec(memory_space=pltpu.HBM)] * 5,
            out_specs=pl.BlockSpec(memory_space=pltpu.VMEM),
            scratch_shapes=[
                pltpu.VMEM((1, E * B), F32),
                pltpu.VMEM(diag.shape, diag.dtype),
                pltpu.VMEM(faces.shape, faces.dtype),
                pltpu.VMEM(precond.shape, precond.dtype),
                pltpu.SMEM(neighbours.shape, neighbours.dtype),
                pltpu.SemaphoreType.DMA((5,)),
                pltpu.VMEM((2, subs + 1, E, LANES), F32),
                pltpu.VMEM((2, subs + 1, E, LANES), F32),
                pltpu.VMEM((CHIPS_X * subs, LANES), F32),
                pltpu.VMEM((chips_z, LANES), F32),
                pltpu.VMEM((1, LANES), F32),
                pltpu.VMEM((1, LANES), F32),
                pltpu.SemaphoreType.DMA((2,)),
                pltpu.SemaphoreType.DMA((2,)),
                pltpu.SemaphoreType.DMA((2,)),
                pltpu.SemaphoreType.DMA((2,)),
                pltpu.SemaphoreType.REGULAR,
                pltpu.SemaphoreType.REGULAR,
                pltpu.SemaphoreType.REGULAR,
            ],
            compiler_params=pltpu.CompilerParams(
                collective_id=0, has_side_effects=True, vmem_limit_bytes=62 * 2**20
            ),
            cost_estimate=pl.CostEstimate(flops=2_000_000, bytes_accessed=500_000, transcendentals=0),
        )(rhs.reshape(1, -1), diag, faces, precond, neighbours)
        return out.reshape(-1)

    rows = P(("dom", "sub"), None)
    flat = P(("dom", "sub"))
    return jax.shard_map(
        body, mesh=mesh, in_specs=(flat, rows, rows, rows, rows), out_specs=flat, check_vma=False
    )
```

```python
import functools

import jax
import jax.numpy as jnp
from jax import lax
from jax.experimental import pallas as pl
from jax.experimental.pallas import tpu as pltpu
from jax.sharding import PartitionSpec as P

B = 100
E = 4
LANES = 128
TILES = 25
CHIPS_X = 4
SCALES = (2.0**-44, 1.0, 2.0**44)
SHRINK = 2.0**-12
MESH = pl.DeviceIdType.MESH
F32 = jnp.float32


def lane_of(rows=E):
    return lax.broadcasted_iota(jnp.int32, (rows, LANES), 1)


def periodic(vector):
    lane = lane_of()
    base = jnp.where(lane < B, vector, pltpu.roll(vector, B, 1))
    tiles = []
    for j in range(TILES):
        offset = 28 * j % B
        if offset == 0:
            tiles.append(base)
        else:
            left = pltpu.roll(base, LANES - offset, 1)
            right = pltpu.roll(base, B - offset, 1)
            tiles.append(jnp.where(lane < LANES - offset, left, right))
    return tiles


def tile_at(ref, j):
    width = min(LANES, ref.shape[1] - j * LANES)
    part = ref[:, j * LANES : j * LANES + width].astype(F32)
    if width < LANES:
        part = jnp.concatenate([part, jnp.zeros((E, LANES - width), F32)], axis=1)
    return part


def row_products(ref, vector):
    lane = lane_of()
    tiles = periodic(vector)
    count = -(-B * B // LANES)
    products = [tile_at(ref, j) * tiles[j % TILES] for j in range(count)]
    sums = []
    for a in range(B):
        j, start = divmod(B * a, LANES)
        if start + B <= LANES:
            row = products[j]
            if start > 0:
                row = jnp.where(lane >= start, row, 0.0)
            if start + B < LANES:
                row = jnp.where(lane < start + B, row, 0.0)
        else:
            row = jnp.where(lane >= start, products[j], jnp.where(lane < start + B - LANES, products[j + 1], 0.0))
        sums.append(jnp.sum(row, axis=1, keepdims=True))
    return sums


def fold(tiles):
    lane = lane_of()
    flat = jnp.concatenate(tiles, axis=1)
    width = TILES * LANES
    while width > B:
        width //= 2
        flat = flat[:, :width] + flat[:, width : 2 * width]
    return jnp.concatenate([flat, jnp.zeros((E, LANES - B), F32)], axis=1)


def column_products(ref, first_row, values):
    lane = lane_of()
    start, stop = first_row * B, (first_row + B) * B
    sums = [None] * TILES
    wide = [jnp.broadcast_to(value, (E, LANES)) for value in values]
    for j in range(start // LANES, -(-stop // LANES)):
        factor = None
        for row in range(j * LANES // B, (j * LANES + LANES - 1) // B + 1):
            begin = row * B - j * LANES
            inside = first_row <= row < first_row + B
            value = wide[row - first_row] if inside else jnp.zeros((E, LANES), F32)
            factor = value if factor is None else jnp.where(lane >= begin, value, factor)
        term = tile_at(ref, j) * factor
        slot = j % TILES
        sums[slot] = term if sums[slot] is None else sums[slot] + term
    return fold(sums)


def as_rows(values):
    lane = lane_of()
    out = jnp.zeros((E, LANES), F32)
    for a, value in enumerate(values):
        out = jnp.where(lane == a, value, out)
    return out


def kernel(
    sizes, rhs_hbm, diag_hbm, face_hbm, prec_hbm, near_hbm, out_ref,
    rhs_ref, diag_ref, face_ref, prec_ref, near_ref, load_sem,
    inner_out, outer_out, inner_one, outer_one, inner_two, outer_two, rhs_box, own_box, own_out, sum_box, sum_out,
    sems, known_a, known_b, known_c, known_d,
):
    doms, subs = sizes
    chips_z = doms // CHIPS_X
    d, s = lax.axis_index("dom"), lax.axis_index("sub")
    x, z = d // chips_z, d % chips_z
    slab = subs * E

    loads = [
        pltpu.make_async_copy(src, dst, load_sem.at[i])
        for i, (src, dst) in enumerate(
            [
                (rhs_hbm, rhs_ref), (prec_hbm, prec_ref), (face_hbm, face_ref), (near_hbm, near_ref),
                (diag_hbm, diag_ref),
            ]
        )
    ]
    for load in loads:
        load.start()

    mates = [(s + k) % subs for k in range(subs)]
    rows_x = [(x + k) % CHIPS_X * chips_z for k in range(CHIPS_X)]
    rows_z = [(z + k) % chips_z for k in range(chips_z)]
    far_first = sorted(range(1, subs), key=lambda k: -min(k // 2, subs // 2 - k // 2))
    above, below = (d + 1) % doms, (d + doms - 1) % doms

    def along_z(step):
        return rows_x[0] + rows_z[step % chips_z], s

    def along_x(step):
        return rows_x[step % CHIPS_X] + z, s

    barrier = pltpu.get_barrier_semaphore()

    def tell(semaphore, devices):
        for device in devices:
            pl.semaphore_signal(semaphore, inc=1, device_id=device, device_id_type=MESH)

    beside = [(above, s), (below, s), along_z(1), along_z(-1), along_x(1), along_x(-1)]
    tell(barrier, [(d, mates[k]) for k in far_first] + beside)

    def tell_a():
        tell(known_a, beside)

    def tell_b():
        pl.semaphore_wait(known_a, len(beside))
        tell(known_b, [along_z(2), along_z(-2), along_z(1), along_z(-1)])

    def tell_c():
        pl.semaphore_wait(known_b, 4)
        tell(known_c, [along_z(4), along_z(-4)])

    def tell_d():
        pl.semaphore_wait(known_c, 2)
        tell(known_d, [along_z(2), along_z(-2)])

    def send(src, dst, device, group):
        pltpu.make_async_remote_copy(
            src_ref=src,
            dst_ref=dst,
            send_sem=sems.at[group, 0],
            recv_sem=sems.at[group, 1],
            device_id=device,
            device_id_type=MESH,
        ).start()

    filled = [
        inner_one, outer_one, inner_two, outer_two, rhs_box.at[pl.ds(0, subs - 1)], own_box.at[pl.ds(0, subs - 1)],
        sum_box.at[pl.ds(1, doms - 1)],
    ]
    INNER_ONE, OUTER_ONE, INNER_TWO, OUTER_TWO, RHS, OWN, SUM = range(7)

    def arrived(*groups):
        for group in groups:
            pltpu.make_async_copy(filled[group], filled[group], sems.at[group, 1]).wait()

    loads[3].wait()
    goal = {}
    for e in range(E):
        for face in range(4):
            near = near_ref[e, face]
            row = near - d * slab if face >= 2 else near % E + (E if face == 0 else 0)
            goal[e, face] = jnp.where(near >= 0, row, -1)

    def placed(rows, faces, sent):
        row = lax.broadcasted_iota(jnp.int32, (rows, LANES), 0)
        out = jnp.zeros((rows, LANES), F32)
        for face in faces:
            for e in range(E):
                out = out + jnp.where(row == goal[e, face], sent[face][e : e + 1], 0.0)
        return out

    def outer_of(values):
        sent = {face: column_products(face_ref, face * B, values) for face in (0, 1)}
        return placed(2 * E, (0, 1), sent)

    def inner_of(values):
        sent = {face: column_products(face_ref, face * B, values) for face in (2, 3)}
        return placed(slab, (2, 3), sent)

    def store_slab(ref, value):
        for k in range(subs):
            ref[k] = value[E * k : E * k + E]

    loads[0].wait()
    flat = jnp.concatenate([rhs_ref[...] * SHRINK, jnp.zeros((1, E * LANES - E * B), F32)], axis=1)
    start = jnp.concatenate([flat[:, B * e : B * e + B] for e in range(E)], axis=0)
    start = jnp.concatenate([start, jnp.zeros((E, LANES - B), F32)], axis=1)
    rhs_box[s] = start

    loads[1].wait()
    values = row_products(prec_ref, start)
    loads[2].wait()
    store_slab(inner_out.at[0], inner_of(values))
    outer = outer_of(values)
    outer_out[0, 0] = outer[:E]
    outer_out[0, 1] = outer[E:]
    pl.semaphore_wait(barrier, subs - 1 + len(beside))
    for k in far_first:
        send(inner_out.at[0, mates[k]], inner_one.at[k - 1], (d, mates[k]), INNER_ONE)
    send(outer_out.at[0, 0], outer_one.at[0], (above, s), OUTER_ONE)
    send(outer_out.at[0, 1], outer_one.at[1], (below, s), OUTER_ONE)
    tell_a()
    for k in far_first:
        send(rhs_box.at[s], rhs_box.at[s], (d, mates[k]), RHS)
    loads[4].wait()
    image = inner_out[0, s] + column_products(diag_ref, 0, values)
    search_one = as_rows(values)
    tell_b()
    tell_c()
    arrived(INNER_ONE, OUTER_ONE)
    for k in range(subs - 1):
        image = image + inner_one[k]
    image = image + outer_one[0] + outer_one[1]

    values = row_products(prec_ref, image)
    outer = outer_of(values)
    outer_out[1, 0] = outer[:E]
    outer_out[1, 1] = outer[E:]
    for k in far_first + [0]:
        send(outer_out.at[1, 0], outer_two.at[0, s], (above, mates[k]), OUTER_TWO)
        send(outer_out.at[1, 1], outer_two.at[1, s], (below, mates[k]), OUTER_TWO)
    store_slab(inner_out.at[1], inner_of(values))
    for k in far_first:
        send(inner_out.at[1], inner_two.at[k - 1], (d, mates[k]), INNER_TWO)
    own_out[0] = image
    own_out[1] = column_products(diag_ref, 0, values)
    for k in far_first:
        send(own_out, own_box.at[s], (d, mates[k]), OWN)
    own_box[s] = own_out[...]
    search_two = as_rows(values)
    tell_d()
    arrived(RHS, OUTER_TWO, INNER_TWO, OWN)

    products = []
    for k in range(subs):
        rhs, one = rhs_box[k], own_box[k, 0]
        two = own_box[k, 1] + outer_two[0, k] + outer_two[1, k] + inner_out[1, k]
        for m in range(subs - 1):
            two = two + inner_two[m, k]
        terms = [one * rhs, two * rhs]
        for scale in SCALES:
            low_one, low_two = one * scale, two * (scale * scale)
            terms += [low_one * low_one, low_one * low_two, low_two * low_two]
        products = [a + b for a, b in zip(products, terms)] if products else terms
    lane = lane_of(1)
    row = lax.broadcasted_iota(jnp.int32, (16, LANES), 0)
    table = jnp.zeros((16, LANES), F32)
    for q, product in enumerate(products):
        table = jnp.where(row == q, jnp.sum(product, axis=0, keepdims=True), table)
    table = jnp.where(row == lane_of(16), jnp.sum(table, axis=1, keepdims=True), 0.0)
    message = jnp.sum(table, axis=0, keepdims=True)

    pl.semaphore_wait(known_d, 2)
    sum_out[...] = message
    sum_box[0:1] = message
    for k_z in sorted(range(chips_z), key=lambda k: -min(k, chips_z - k)):
        for k_x in sorted(range(CHIPS_X), key=lambda k: -min(k, CHIPS_X - k)):
            k = k_x * chips_z + k_z
            if k:
                send(sum_out, sum_box.at[pl.ds(k, 1)], (rows_x[k_x] + rows_z[k_z], s), SUM)
    arrived(SUM)
    message = jnp.sum(sum_box[...], axis=0, keepdims=True)

    def entry(q):
        return jnp.sum(jnp.where(lane == q, message, 0.0), axis=1, keepdims=True)

    def pick(q):
        low, mid, high = (entry(2 + 3 * i + q) for i in range(3))
        return jnp.where(too_large, low, jnp.where(too_small, high, mid))

    size = entry(2 + 3 + 2)
    too_large = jnp.logical_not(size < 1e26)
    too_small = size < 1e-26
    scale = jnp.where(too_large, SCALES[0], jnp.where(too_small, SCALES[2], SCALES[1]))
    one_one, one_two, two_two = pick(0), pick(1), pick(2)
    one_rhs, two_rhs = entry(0) * scale, entry(1) * scale * scale
    slope = one_two / one_one
    rest = jnp.maximum(two_two - slope * one_two, two_two * 2.0**-22)
    second = (two_rhs - slope * one_rhs) / rest
    first = one_rhs / one_one - slope * second
    answer = first * scale * (search_one * (1.0 / SHRINK)) + second * scale * scale * (search_two * (1.0 / SHRINK))
    out_ref[...] = jnp.concatenate([answer[e : e + 1, :B] for e in range(E)], axis=1)

    for group, ref in enumerate(filled):
        pltpu.make_async_copy(ref, ref, sems.at[group, 0]).wait()


def solution(mesh):
    doms, subs = mesh.shape["dom"], mesh.shape["sub"]

    def body(rhs, diag, faces, precond, neighbours):
        out = pl.pallas_call(
            functools.partial(kernel, (doms, subs)),
            out_shape=pltpu.VMEM((1, E * B), F32),
            in_specs=[pl.BlockSpec(memory_space=pltpu.HBM)] * 5,
            out_specs=pl.BlockSpec(memory_space=pltpu.VMEM),
            scratch_shapes=[
                pltpu.VMEM((1, E * B), F32),
                pltpu.VMEM(diag.shape, diag.dtype),
                pltpu.VMEM(faces.shape, faces.dtype),
                pltpu.VMEM(precond.shape, precond.dtype),
                pltpu.SMEM(neighbours.shape, neighbours.dtype),
                pltpu.SemaphoreType.DMA((5,)),
                pltpu.VMEM((2, subs, E, LANES), F32),
                pltpu.VMEM((2, 2, E, LANES), F32),
                pltpu.VMEM((subs - 1, E, LANES), F32),
                pltpu.VMEM((2, E, LANES), F32),
                pltpu.VMEM((subs - 1, subs, E, LANES), F32),
                pltpu.VMEM((2, subs, E, LANES), F32),
                pltpu.VMEM((subs, E, LANES), F32),
                pltpu.VMEM((subs, 2, E, LANES), F32),
                pltpu.VMEM((2, E, LANES), F32),
                pltpu.VMEM((doms, LANES), F32),
                pltpu.VMEM((1, LANES), F32),
                pltpu.SemaphoreType.DMA((7, 2)),
                pltpu.SemaphoreType.REGULAR,
                pltpu.SemaphoreType.REGULAR,
                pltpu.SemaphoreType.REGULAR,
                pltpu.SemaphoreType.REGULAR,
            ],
            compiler_params=pltpu.CompilerParams(
                collective_id=0, has_side_effects=True, vmem_limit_bytes=62 * 2**20
            ),
            cost_estimate=pl.CostEstimate(flops=2_000_000, bytes_accessed=500_000, transcendentals=0),
        )(rhs.reshape(1, -1), diag, faces, precond, neighbours)
        return out.reshape(-1)

    rows = P(("dom", "sub"), None)
    flat = P(("dom", "sub"))
    return jax.shard_map(
        body, mesh=mesh, in_specs=(flat, rows, rows, rows, rows), out_specs=flat, check_vma=False
    )
```

```python
import functools

import jax
import jax.numpy as jnp
from jax import lax
from jax.experimental import pallas as pl
from jax.experimental.pallas import tpu as pltpu
from jax.sharding import PartitionSpec as P

B = 100
E = 4
LANES = 128
TILES = 25
CHIPS_X = 4
SCALES = (2.0**-44, 1.0, 2.0**44)
SHRINK = 2.0**-12
MESH = pl.DeviceIdType.MESH
F32 = jnp.float32


def lane_of(rows=E):
    return lax.broadcasted_iota(jnp.int32, (rows, LANES), 1)


def periodic(vector):
    lane = lane_of()
    base = jnp.where(lane < B, vector, pltpu.roll(vector, B, 1))
    tiles = []
    for j in range(TILES):
        offset = 28 * j % B
        if offset == 0:
            tiles.append(base)
        else:
            left = pltpu.roll(base, LANES - offset, 1)
            right = pltpu.roll(base, B - offset, 1)
            tiles.append(jnp.where(lane < LANES - offset, left, right))
    return tiles


def tile_at(ref, j):
    width = min(LANES, ref.shape[1] - j * LANES)
    part = ref[:, j * LANES : j * LANES + width].astype(F32)
    if width < LANES:
        part = jnp.concatenate([part, jnp.zeros((E, LANES - width), F32)], axis=1)
    return part


def row_products(ref, vector):
    lane = lane_of()
    tiles = periodic(vector)
    count = -(-B * B // LANES)
    products = [tile_at(ref, j) * tiles[j % TILES] for j in range(count)]
    sums = []
    for a in range(B):
        j, start = divmod(B * a, LANES)
        if start + B <= LANES:
            row = products[j]
            if start > 0:
                row = jnp.where(lane >= start, row, 0.0)
            if start + B < LANES:
                row = jnp.where(lane < start + B, row, 0.0)
        else:
            row = jnp.where(lane >= start, products[j], jnp.where(lane < start + B - LANES, products[j + 1], 0.0))
        sums.append(jnp.sum(row, axis=1, keepdims=True))
    return sums


def fold(tiles):
    lane = lane_of()
    flat = jnp.concatenate(tiles, axis=1)
    width = TILES * LANES
    while width > B:
        width //= 2
        flat = flat[:, :width] + flat[:, width : 2 * width]
    return jnp.concatenate([flat, jnp.zeros((E, LANES - B), F32)], axis=1)


def column_products(ref, first_row, values):
    lane = lane_of()
    start, stop = first_row * B, (first_row + B) * B
    sums = [None] * TILES
    wide = [jnp.broadcast_to(value, (E, LANES)) for value in values]
    for j in range(start // LANES, -(-stop // LANES)):
        factor = None
        for row in range(j * LANES // B, (j * LANES + LANES - 1) // B + 1):
            begin = row * B - j * LANES
            inside = first_row <= row < first_row + B
            value = wide[row - first_row] if inside else jnp.zeros((E, LANES), F32)
            factor = value if factor is None else jnp.where(lane >= begin, value, factor)
        term = tile_at(ref, j) * factor
        slot = j % TILES
        sums[slot] = term if sums[slot] is None else sums[slot] + term
    return fold(sums)


def unfold(ref, row):
    j, start = divmod(row * B, LANES)
    part = tile_at(ref, j)
    if start + B > LANES:
        part = jnp.where(lane_of() >= start, part, tile_at(ref, j + 1))
    return pltpu.roll(part, LANES - start, 1) if start else part


def weighted(ref, values, rows):
    sums = [None] * 4
    for a, value in enumerate(values):
        term = ref[a] * value[:rows]
        sums[a % 4] = term if sums[a % 4] is None else sums[a % 4] + term
    return jnp.where(lane_of(rows) < B, (sums[0] + sums[1]) + (sums[2] + sums[3]), 0.0)


def as_rows(values):
    lane = lane_of()
    out = jnp.zeros((E, LANES), F32)
    for a, value in enumerate(values):
        out = jnp.where(lane == a, value[:E], out)
    return out


def kernel(
    sizes, rhs_hbm, diag_hbm, face_hbm, prec_hbm, near_hbm, out_ref,
    rhs_ref, diag_ref, face_ref, prec_ref, near_ref, prec_rows, diag_rows, outer_rows, inner_rows, load_sem,
    inner_out, outer_out, inner_one, outer_one, inner_two, outer_two, rhs_box, own_box, own_out, sum_box, sum_out,
    sems, known_a, known_b, known_c, known_d,
):
    doms, subs = sizes
    chips_z = doms // CHIPS_X
    d, s = lax.axis_index("dom"), lax.axis_index("sub")
    x, z = d // chips_z, d % chips_z
    slab = subs * E

    loads = [
        pltpu.make_async_copy(src, dst, load_sem.at[i])
        for i, (src, dst) in enumerate(
            [
                (rhs_hbm, rhs_ref), (prec_hbm, prec_ref), (face_hbm, face_ref), (near_hbm, near_ref),
                (diag_hbm, diag_ref),
            ]
        )
    ]
    mates = [(s + k) % subs for k in range(subs)]
    rows_x = [(x + k) % CHIPS_X * chips_z for k in range(CHIPS_X)]
    rows_z = [(z + k) % chips_z for k in range(chips_z)]
    far_first = sorted(range(1, subs), key=lambda k: -min(k // 2, subs // 2 - k // 2))
    above, below = (d + 1) % doms, (d + doms - 1) % doms

    def along_z(step):
        return rows_x[0] + rows_z[step % chips_z], s

    def along_x(step):
        return rows_x[step % CHIPS_X] + z, s

    barrier = pltpu.get_barrier_semaphore()

    def tell(semaphore, devices):
        for device in devices:
            pl.semaphore_signal(semaphore, inc=1, device_id=device, device_id_type=MESH)

    beside = [(above, s), (below, s), along_z(1), along_z(-1), along_x(1), along_x(-1)]
    tell(barrier, [(d, mates[k]) for k in far_first])
    for load in loads:
        load.start()
    tell(barrier, beside)

    def tell_a():
        tell(known_a, beside)

    def tell_b():
        pl.semaphore_wait(known_a, len(beside))
        tell(known_b, [along_z(2), along_z(-2), along_z(1), along_z(-1)])

    def tell_c():
        pl.semaphore_wait(known_b, 4)
        tell(known_c, [along_z(4), along_z(-4)])

    def tell_d():
        pl.semaphore_wait(known_c, 2)
        tell(known_d, [along_z(2), along_z(-2)])

    def send(src, dst, device, group):
        pltpu.make_async_remote_copy(
            src_ref=src,
            dst_ref=dst,
            send_sem=sems.at[group, 0],
            recv_sem=sems.at[group, 1],
            device_id=device,
            device_id_type=MESH,
        ).start()

    filled = [
        inner_one, outer_one, inner_two, outer_two, rhs_box.at[pl.ds(0, subs - 1)], own_box.at[pl.ds(0, subs - 1)],
        sum_box.at[pl.ds(1, doms - 1)],
    ]
    INNER_ONE, OUTER_ONE, INNER_TWO, OUTER_TWO, RHS, OWN, SUM = range(7)

    def arrived(*groups):
        for group in groups:
            pltpu.make_async_copy(filled[group], filled[group], sems.at[group, 1]).wait()

    loads[3].wait()
    goal = {}
    for e in range(E):
        for face in range(4):
            near = near_ref[e, face]
            row = near - d * slab if face >= 2 else near % E + (E if face == 0 else 0)
            goal[e, face] = jnp.where(near >= 0, row, -1)

    def placed(rows, faces, sent):
        row = lax.broadcasted_iota(jnp.int32, (rows, LANES), 0)
        out = jnp.zeros((rows, LANES), F32)
        for i, face in enumerate(faces):
            for e in range(E):
                out = out + jnp.where(row == goal[e, face], sent[E * i + e : E * i + e + 1], 0.0)
        return out

    def pair_products(faces, values):
        return jnp.concatenate([column_products(face_ref, face * B, values) for face in faces], axis=0)

    def store_slab(ref, value):
        for k in range(subs):
            ref[k] = value[E * k : E * k + E]

    loads[0].wait()
    flat = jnp.concatenate([rhs_ref[...] * SHRINK, jnp.zeros((1, E * LANES - E * B), F32)], axis=1)
    start = jnp.concatenate([flat[:, B * e : B * e + B] for e in range(E)], axis=0)
    start = jnp.concatenate([start, jnp.zeros((E, LANES - B), F32)], axis=1)
    rhs_box[s] = start

    loads[1].wait()
    values = row_products(prec_ref, start)
    loads[2].wait()
    store_slab(inner_out.at[0], placed(slab, (2, 3), pair_products((2, 3), values)))
    pl.semaphore_wait(barrier, subs - 1 + len(beside))
    for k in far_first:
        send(inner_out.at[0, mates[k]], inner_one.at[k - 1], (d, mates[k]), INNER_ONE)
    outer = placed(2 * E, (0, 1), pair_products((0, 1), values))
    outer_out[0, 0] = outer[:E]
    outer_out[0, 1] = outer[E:]
    send(outer_out.at[0, 0], outer_one.at[0], (above, s), OUTER_ONE)
    send(outer_out.at[0, 1], outer_one.at[1], (below, s), OUTER_ONE)
    tell_a()
    for k in far_first:
        send(rhs_box.at[s], rhs_box.at[s], (d, mates[k]), RHS)
    loads[4].wait()
    image = inner_out[0, s] + column_products(diag_ref, 0, values)
    search_one = as_rows(values)

    for a in range(B):
        row = unfold(prec_ref, a)
        prec_rows[a] = jnp.concatenate([row, row], axis=0)
        diag_rows[a] = unfold(diag_ref, a)
        outer_rows[a] = jnp.concatenate([unfold(face_ref, a), unfold(face_ref, B + a)], axis=0)
        inner_rows[a] = jnp.concatenate([unfold(face_ref, 2 * B + a), unfold(face_ref, 3 * B + a)], axis=0)
    tell_b()
    tell_c()
    arrived(INNER_ONE, OUTER_ONE)
    for k in range(subs - 1):
        image = image + inner_one[k]
    image = image + outer_one[0] + outer_one[1]

    twice = jnp.concatenate([image, image], axis=0)
    values = [jnp.sum(prec_rows[a] * twice, axis=1, keepdims=True) for a in range(B)]
    outer = placed(2 * E, (0, 1), weighted(outer_rows, values, 2 * E))
    outer_out[1, 0] = outer[:E]
    outer_out[1, 1] = outer[E:]
    for k in far_first + [0]:
        send(outer_out.at[1, 0], outer_two.at[0, s], (above, mates[k]), OUTER_TWO)
        send(outer_out.at[1, 1], outer_two.at[1, s], (below, mates[k]), OUTER_TWO)
    store_slab(inner_out.at[1], placed(slab, (2, 3), weighted(inner_rows, values, 2 * E)))
    for k in far_first:
        send(inner_out.at[1], inner_two.at[k - 1], (d, mates[k]), INNER_TWO)
    own_out[0] = image
    own_out[1] = weighted(diag_rows, values, E)
    for k in far_first:
        send(own_out, own_box.at[s], (d, mates[k]), OWN)
    own_box[s] = own_out[...]
    search_two = as_rows(values)
    tell_d()
    arrived(RHS, OUTER_TWO, INNER_TWO, OWN)

    products = []
    for k in range(subs):
        rhs, one = rhs_box[k], own_box[k, 0]
        two = own_box[k, 1] + outer_two[0, k] + outer_two[1, k] + inner_out[1, k]
        for m in range(subs - 1):
            two = two + inner_two[m, k]
        terms = [one * rhs, two * rhs]
        for scale in SCALES:
            low_one, low_two = one * scale, two * (scale * scale)
            terms += [low_one * low_one, low_one * low_two, low_two * low_two]
        products = [a + b for a, b in zip(products, terms)] if products else terms
    lane = lane_of(1)
    row = lax.broadcasted_iota(jnp.int32, (16, LANES), 0)
    table = jnp.zeros((16, LANES), F32)
    for q, product in enumerate(products):
        table = jnp.where(row == q, jnp.sum(product, axis=0, keepdims=True), table)
    table = jnp.where(row == lane_of(16), jnp.sum(table, axis=1, keepdims=True), 0.0)
    message = jnp.sum(table, axis=0, keepdims=True)

    pl.semaphore_wait(known_d, 2)
    sum_out[...] = message
    sum_box[0:1] = message
    for k_z in sorted(range(chips_z), key=lambda k: -min(k, chips_z - k)):
        for k_x in sorted(range(CHIPS_X), key=lambda k: -min(k, CHIPS_X - k)):
            k = k_x * chips_z + k_z
            if k:
                send(sum_out, sum_box.at[pl.ds(k, 1)], (rows_x[k_x] + rows_z[k_z], s), SUM)
    arrived(SUM)
    message = jnp.sum(sum_box[...], axis=0, keepdims=True)

    def entry(q):
        return jnp.sum(jnp.where(lane == q, message, 0.0), axis=1, keepdims=True)

    def pick(q):
        low, mid, high = (entry(2 + 3 * i + q) for i in range(3))
        return jnp.where(too_large, low, jnp.where(too_small, high, mid))

    size = entry(2 + 3 + 2)
    too_large = jnp.logical_not(size < 1e26)
    too_small = size < 1e-26
    scale = jnp.where(too_large, SCALES[0], jnp.where(too_small, SCALES[2], SCALES[1]))
    one_one, one_two, two_two = pick(0), pick(1), pick(2)
    one_rhs, two_rhs = entry(0) * scale, entry(1) * scale * scale
    slope = one_two / one_one
    rest = jnp.maximum(two_two - slope * one_two, two_two * 2.0**-22)
    second = (two_rhs - slope * one_rhs) / rest
    first = one_rhs / one_one - slope * second
    answer = first * scale * (search_one * (1.0 / SHRINK)) + second * scale * scale * (search_two * (1.0 / SHRINK))
    out_ref[...] = jnp.concatenate([answer[e : e + 1, :B] for e in range(E)], axis=1)

    for group, ref in enumerate(filled):
        pltpu.make_async_copy(ref, ref, sems.at[group, 0]).wait()


def solution(mesh):
    doms, subs = mesh.shape["dom"], mesh.shape["sub"]

    def body(rhs, diag, faces, precond, neighbours):
        out = pl.pallas_call(
            functools.partial(kernel, (doms, subs)),
            out_shape=pltpu.VMEM((1, E * B), F32),
            in_specs=[pl.BlockSpec(memory_space=pltpu.HBM)] * 5,
            out_specs=pl.BlockSpec(memory_space=pltpu.VMEM),
            scratch_shapes=[
                pltpu.VMEM((1, E * B), F32),
                pltpu.VMEM(diag.shape, diag.dtype),
                pltpu.VMEM(faces.shape, faces.dtype),
                pltpu.VMEM(precond.shape, precond.dtype),
                pltpu.SMEM(neighbours.shape, neighbours.dtype),
                pltpu.VMEM((B, 2 * E, LANES), F32),
                pltpu.VMEM((B, E, LANES), F32),
                pltpu.VMEM((B, 2 * E, LANES), F32),
                pltpu.VMEM((B, 2 * E, LANES), F32),
                pltpu.SemaphoreType.DMA((5,)),
                pltpu.VMEM((2, subs, E, LANES), F32),
                pltpu.VMEM((2, 2, E, LANES), F32),
                pltpu.VMEM((subs - 1, E, LANES), F32),
                pltpu.VMEM((2, E, LANES), F32),
                pltpu.VMEM((subs - 1, subs, E, LANES), F32),
                pltpu.VMEM((2, subs, E, LANES), F32),
                pltpu.VMEM((subs, E, LANES), F32),
                pltpu.VMEM((subs, 2, E, LANES), F32),
                pltpu.VMEM((2, E, LANES), F32),
                pltpu.VMEM((doms, LANES), F32),
                pltpu.VMEM((1, LANES), F32),
                pltpu.SemaphoreType.DMA((7, 2)),
                pltpu.SemaphoreType.REGULAR,
                pltpu.SemaphoreType.REGULAR,
                pltpu.SemaphoreType.REGULAR,
                pltpu.SemaphoreType.REGULAR,
            ],
            compiler_params=pltpu.CompilerParams(
                collective_id=0, has_side_effects=True, vmem_limit_bytes=62 * 2**20
            ),
            cost_estimate=pl.CostEstimate(flops=2_000_000, bytes_accessed=500_000, transcendentals=0),
        )(rhs.reshape(1, -1), diag, faces, precond, neighbours)
        return out.reshape(-1)

    rows = P(("dom", "sub"), None)
    flat = P(("dom", "sub"))
    return jax.shard_map(
        body, mesh=mesh, in_specs=(flat, rows, rows, rows, rows), out_specs=flat, check_vma=False
    )
```

```python
import functools

import jax
import jax.numpy as jnp
from jax import lax
from jax.experimental import pallas as pl
from jax.experimental.pallas import tpu as pltpu
from jax.sharding import PartitionSpec as P

B = 100
E = 4
LANES = 128
TILES = 25
CHIPS_X = 4
SCALES = (2.0**-44, 1.0, 2.0**44)
SHRINK = 2.0**-12
MESH = pl.DeviceIdType.MESH
F32 = jnp.float32


def lane_of(rows=E):
    return lax.broadcasted_iota(jnp.int32, (rows, LANES), 1)


def periodic(vector):
    lane = lane_of()
    base = jnp.where(lane < B, vector, pltpu.roll(vector, B, 1))
    rolled = {LANES: base}
    for shift in range(4, LANES, 4):
        rolled[shift] = pltpu.roll(base, shift, 1)
    tiles = []
    for j in range(TILES):
        offset = 28 * j % B
        tiles.append(jnp.where(lane < LANES - offset, rolled[LANES - offset], rolled[B - offset]))
    return tiles


def tile_at(ref, j):
    width = min(LANES, ref.shape[1] - j * LANES)
    part = ref[:, j * LANES : j * LANES + width].astype(F32)
    if width < LANES:
        part = jnp.concatenate([part, jnp.zeros((E, LANES - width), F32)], axis=1)
    return part


def row_products(ref, vector):
    lane = lane_of()
    tiles = periodic(vector)
    count = -(-B * B // LANES)
    products = [tile_at(ref, j) * tiles[j % TILES] for j in range(count)]
    sums = []
    for a in range(B):
        j, start = divmod(B * a, LANES)
        if start + B <= LANES:
            row = products[j]
            if start > 0:
                row = jnp.where(lane >= start, row, 0.0)
            if start + B < LANES:
                row = jnp.where(lane < start + B, row, 0.0)
        else:
            row = jnp.where(lane >= start, products[j], jnp.where(lane < start + B - LANES, products[j + 1], 0.0))
        sums.append(jnp.sum(row, axis=1, keepdims=True))
    return sums


def fold(tiles):
    lane = lane_of()
    sums = [None] * 4
    for row in range(TILES * LANES // B):
        j, start = divmod(row * B, LANES)
        part = tiles[j]
        if start + B > LANES:
            part = jnp.where(lane >= start, part, tiles[j + 1])
        if start:
            part = pltpu.roll(part, LANES - start, 1)
        sums[row % 4] = part if sums[row % 4] is None else sums[row % 4] + part
    return jnp.where(lane < B, (sums[0] + sums[1]) + (sums[2] + sums[3]), 0.0)


def column_products(ref, first_row, values):
    lane = lane_of()
    start, stop = first_row * B, (first_row + B) * B
    sums = [None] * TILES
    wide = [jnp.broadcast_to(value, (E, LANES)) for value in values]
    for j in range(start // LANES, -(-stop // LANES)):
        factor = None
        for row in range(j * LANES // B, (j * LANES + LANES - 1) // B + 1):
            begin = row * B - j * LANES
            inside = first_row <= row < first_row + B
            value = wide[row - first_row] if inside else jnp.zeros((E, LANES), F32)
            factor = value if factor is None else jnp.where(lane >= begin, value, factor)
        term = tile_at(ref, j) * factor
        slot = j % TILES
        sums[slot] = term if sums[slot] is None else sums[slot] + term
    return fold(sums)


def unfold(ref, row):
    j, start = divmod(row * B, LANES)
    part = tile_at(ref, j)
    if start + B > LANES:
        part = jnp.where(lane_of() >= start, part, tile_at(ref, j + 1))
    return pltpu.roll(part, LANES - start, 1) if start else part


def weighted(ref, values, rows):
    sums = [None] * 4
    for a, value in enumerate(values):
        term = ref[a] * value[:rows]
        sums[a % 4] = term if sums[a % 4] is None else sums[a % 4] + term
    return jnp.where(lane_of(rows) < B, (sums[0] + sums[1]) + (sums[2] + sums[3]), 0.0)


def as_rows(values):
    lane = lane_of()
    out = jnp.zeros((E, LANES), F32)
    for a, value in enumerate(values):
        out = jnp.where(lane == a, value[:E], out)
    return out


def kernel(
    sizes, rhs_hbm, diag_hbm, face_hbm, prec_hbm, near_hbm, out_ref,
    rhs_ref, diag_ref, face_ref, prec_ref, near_ref, prec_rows, diag_rows, outer_rows, inner_rows, load_sem,
    inner_out, outer_out, inner_one, outer_one, inner_two, outer_two, rhs_box, own_box, own_out, sum_box, sum_out,
    sems, known_a, known_b, known_c, known_d,
):
    doms, subs = sizes
    chips_z = doms // CHIPS_X
    d, s = lax.axis_index("dom"), lax.axis_index("sub")
    x, z = d // chips_z, d % chips_z
    slab = subs * E

    split = 2 * B * B // LANES * LANES
    early, late = pl.ds(0, split), pl.ds(split, 4 * B * B - split)
    loads = [
        pltpu.make_async_copy(src, dst, load_sem.at[i])
        for i, (src, dst) in enumerate(
            [
                (rhs_hbm, rhs_ref), (prec_hbm, prec_ref), (face_hbm.at[:, late], face_ref.at[:, late]), (near_hbm, near_ref),
                (diag_hbm, diag_ref), (face_hbm.at[:, early], face_ref.at[:, early]),
            ]
        )
    ]
    mates = [(s + k) % subs for k in range(subs)]
    rows_x = [(x + k) % CHIPS_X * chips_z for k in range(CHIPS_X)]
    rows_z = [(z + k) % chips_z for k in range(chips_z)]
    far_first = sorted(range(1, subs), key=lambda k: -min(k // 2, subs // 2 - k // 2))
    above, below = (d + 1) % doms, (d + doms - 1) % doms

    def along_z(step):
        return rows_x[0] + rows_z[step % chips_z], s

    def along_x(step):
        return rows_x[step % CHIPS_X] + z, s

    barrier = pltpu.get_barrier_semaphore()

    def tell(semaphore, devices):
        for device in devices:
            pl.semaphore_signal(semaphore, inc=1, device_id=device, device_id_type=MESH)

    beside = [(above, s), (below, s), along_z(1), along_z(-1), along_x(1), along_x(-1)]
    tell(barrier, [(d, mates[k]) for k in far_first])
    for load in loads:
        load.start()
    tell(barrier, beside)

    def tell_a():
        tell(known_a, beside)

    def tell_b():
        pl.semaphore_wait(known_a, len(beside))
        tell(known_b, [along_z(2), along_z(-2), along_z(1), along_z(-1)])

    def tell_c():
        pl.semaphore_wait(known_b, 4)
        tell(known_c, [along_z(4), along_z(-4)])

    def tell_d():
        pl.semaphore_wait(known_c, 2)
        tell(known_d, [along_z(2), along_z(-2)])

    def send(src, dst, device, group):
        pltpu.make_async_remote_copy(
            src_ref=src,
            dst_ref=dst,
            send_sem=sems.at[group, 0],
            recv_sem=sems.at[group, 1],
            device_id=device,
            device_id_type=MESH,
        ).start()

    filled = [
        inner_one, outer_one, inner_two, outer_two, rhs_box.at[pl.ds(0, subs - 1)], own_box.at[pl.ds(0, subs - 1)],
        sum_box.at[pl.ds(1, doms - 1)],
    ]
    INNER_ONE, OUTER_ONE, INNER_TWO, OUTER_TWO, RHS, OWN, SUM = range(7)

    def arrived(*groups):
        for group in groups:
            pltpu.make_async_copy(filled[group], filled[group], sems.at[group, 1]).wait()

    goal = {}

    def placed(rows, faces, sent):
        row = lax.broadcasted_iota(jnp.int32, (rows, LANES), 0)
        out = jnp.zeros((rows, LANES), F32)
        for i, face in enumerate(faces):
            for e in range(E):
                out = out + jnp.where(row == goal[e, face], sent[E * i + e : E * i + e + 1], 0.0)
        return out

    def pair_products(faces, values):
        return jnp.concatenate([column_products(face_ref, face * B, values) for face in faces], axis=0)

    def store_slab(ref, value):
        for k in range(subs):
            ref[k] = value[E * k : E * k + E]

    loads[0].wait()
    flat = jnp.concatenate([rhs_ref[...] * SHRINK, jnp.zeros((1, E * LANES - E * B), F32)], axis=1)
    start = jnp.concatenate([flat[:, B * e : B * e + B] for e in range(E)], axis=0)
    start = jnp.concatenate([start, jnp.zeros((E, LANES - B), F32)], axis=1)
    rhs_box[s] = start

    loads[1].wait()
    values = row_products(prec_ref, start)
    loads[2].wait()
    loads[3].wait()
    for e in range(E):
        for face in range(4):
            near = near_ref[e, face]
            row = near - d * slab if face >= 2 else near % E + (E if face == 0 else 0)
            goal[e, face] = jnp.where(near >= 0, row, -1)
    store_slab(inner_out.at[0], placed(slab, (2, 3), pair_products((2, 3), values)))
    pl.semaphore_wait(barrier, subs - 1 + len(beside))
    for k in far_first:
        send(inner_out.at[0, mates[k]], inner_one.at[k - 1], (d, mates[k]), INNER_ONE)
    loads[5].wait()
    outer = placed(2 * E, (0, 1), pair_products((0, 1), values))
    outer_out[0, 0] = outer[:E]
    outer_out[0, 1] = outer[E:]
    send(outer_out.at[0, 0], outer_one.at[0], (above, s), OUTER_ONE)
    send(outer_out.at[0, 1], outer_one.at[1], (below, s), OUTER_ONE)
    tell_a()
    for k in far_first:
        send(rhs_box.at[s], rhs_box.at[s], (d, mates[k]), RHS)
    loads[4].wait()
    image = inner_out[0, s] + column_products(diag_ref, 0, values)
    search_one = as_rows(values)

    for a in range(B):
        row = unfold(prec_ref, a)
        prec_rows[a] = jnp.concatenate([row, row], axis=0)
        diag_rows[a] = unfold(diag_ref, a)
        outer_rows[a] = jnp.concatenate([unfold(face_ref, a), unfold(face_ref, B + a)], axis=0)
        inner_rows[a] = jnp.concatenate([unfold(face_ref, 2 * B + a), unfold(face_ref, 3 * B + a)], axis=0)
    tell_b()
    tell_c()
    arrived(INNER_ONE, OUTER_ONE)
    for k in range(subs - 1):
        image = image + inner_one[k]
    image = image + outer_one[0] + outer_one[1]

    twice = jnp.concatenate([image, image], axis=0)
    values = [jnp.sum(prec_rows[a] * twice, axis=1, keepdims=True) for a in range(B)]
    outer = placed(2 * E, (0, 1), weighted(outer_rows, values, 2 * E))
    outer_out[1, 0] = outer[:E]
    outer_out[1, 1] = outer[E:]
    for k in far_first + [0]:
        send(outer_out.at[1, 0], outer_two.at[0, s], (above, mates[k]), OUTER_TWO)
        send(outer_out.at[1, 1], outer_two.at[1, s], (below, mates[k]), OUTER_TWO)
    store_slab(inner_out.at[1], placed(slab, (2, 3), weighted(inner_rows, values, 2 * E)))
    for k in far_first:
        send(inner_out.at[1], inner_two.at[k - 1], (d, mates[k]), INNER_TWO)
    own_out[0] = image
    own_out[1] = weighted(diag_rows, values, E)
    for k in far_first:
        send(own_out, own_box.at[s], (d, mates[k]), OWN)
    own_box[s] = own_out[...]
    search_two = as_rows(values)
    flat_one, flat_two = (
        jnp.concatenate([rows[e : e + 1, :B] * (1.0 / SHRINK) for e in range(E)], axis=1)
        for rows in (search_one, search_two)
    )
    tell_d()
    arrived(RHS, OUTER_TWO, INNER_TWO, OWN)

    products = []
    for k in range(subs):
        rhs, one = rhs_box[k], own_box[k, 0]
        two = own_box[k, 1] + outer_two[0, k] + outer_two[1, k] + inner_out[1, k]
        for m in range(subs - 1):
            two = two + inner_two[m, k]
        terms = [one * rhs, two * rhs]
        for scale in SCALES:
            low_one, low_two = one * scale, two * (scale * scale)
            terms += [low_one * low_one, low_one * low_two, low_two * low_two]
        products = [a + b for a, b in zip(products, terms)] if products else terms
    lane = lane_of(1)
    row = lax.broadcasted_iota(jnp.int32, (16, LANES), 0)
    table = jnp.zeros((16, LANES), F32)
    for q, product in enumerate(products):
        table = jnp.where(row == q, jnp.sum(product, axis=0, keepdims=True), table)
    table = jnp.where(row == lane_of(16), jnp.sum(table, axis=1, keepdims=True), 0.0)
    message = jnp.sum(table, axis=0, keepdims=True)

    pl.semaphore_wait(known_d, 2)
    sum_out[...] = message
    sum_box[0:1] = message
    for k_z in sorted(range(chips_z), key=lambda k: -min(k, chips_z - k)):
        for k_x in sorted(range(CHIPS_X), key=lambda k: -min(k, CHIPS_X - k)):
            k = k_x * chips_z + k_z
            if k:
                send(sum_out, sum_box.at[pl.ds(k, 1)], (rows_x[k_x] + rows_z[k_z], s), SUM)
    arrived(SUM)
    message = jnp.sum(sum_box[...], axis=0, keepdims=True)

    def entry(q):
        return jnp.sum(jnp.where(lane == q, message, 0.0), axis=1, keepdims=True)

    def pick(q):
        low, mid, high = (entry(2 + 3 * i + q) for i in range(3))
        return jnp.where(too_large, low, jnp.where(too_small, high, mid))

    size = entry(2 + 3 + 2)
    too_large = jnp.logical_not(size < 1e26)
    too_small = size < 1e-26
    scale = jnp.where(too_large, SCALES[0], jnp.where(too_small, SCALES[2], SCALES[1]))
    one_one, one_two, two_two = pick(0), pick(1), pick(2)
    one_rhs, two_rhs = entry(0) * scale, entry(1) * scale * scale
    slope = one_two / one_one
    rest = jnp.maximum(two_two - slope * one_two, two_two * 2.0**-22)
    second = (two_rhs - slope * one_rhs) / rest
    first = one_rhs / one_one - slope * second
    out_ref[...] = first * scale * flat_one + second * scale * scale * flat_two

    for group, ref in enumerate(filled):
        pltpu.make_async_copy(ref, ref, sems.at[group, 0]).wait()


def solution(mesh):
    doms, subs = mesh.shape["dom"], mesh.shape["sub"]

    def body(rhs, diag, faces, precond, neighbours):
        out = pl.pallas_call(
            functools.partial(kernel, (doms, subs)),
            out_shape=pltpu.VMEM((1, E * B), F32),
            in_specs=[pl.BlockSpec(memory_space=pltpu.HBM)] * 5,
            out_specs=pl.BlockSpec(memory_space=pltpu.VMEM),
            scratch_shapes=[
                pltpu.VMEM((1, E * B), F32),
                pltpu.VMEM(diag.shape, diag.dtype),
                pltpu.VMEM(faces.shape, faces.dtype),
                pltpu.VMEM(precond.shape, precond.dtype),
                pltpu.SMEM(neighbours.shape, neighbours.dtype),
                pltpu.VMEM((B, 2 * E, LANES), F32),
                pltpu.VMEM((B, E, LANES), F32),
                pltpu.VMEM((B, 2 * E, LANES), F32),
                pltpu.VMEM((B, 2 * E, LANES), F32),
                pltpu.SemaphoreType.DMA((6,)),
                pltpu.VMEM((2, subs, E, LANES), F32),
                pltpu.VMEM((2, 2, E, LANES), F32),
                pltpu.VMEM((subs - 1, E, LANES), F32),
                pltpu.VMEM((2, E, LANES), F32),
                pltpu.VMEM((subs - 1, subs, E, LANES), F32),
                pltpu.VMEM((2, subs, E, LANES), F32),
                pltpu.VMEM((subs, E, LANES), F32),
                pltpu.VMEM((subs, 2, E, LANES), F32),
                pltpu.VMEM((2, E, LANES), F32),
                pltpu.VMEM((doms, LANES), F32),
                pltpu.VMEM((1, LANES), F32),
                pltpu.SemaphoreType.DMA((7, 2)),
                pltpu.SemaphoreType.REGULAR,
                pltpu.SemaphoreType.REGULAR,
                pltpu.SemaphoreType.REGULAR,
                pltpu.SemaphoreType.REGULAR,
            ],
            compiler_params=pltpu.CompilerParams(
                collective_id=0, has_side_effects=True, vmem_limit_bytes=62 * 2**20
            ),
            cost_estimate=pl.CostEstimate(flops=2_000_000, bytes_accessed=500_000, transcendentals=0),
        )(rhs.reshape(1, -1), diag, faces, precond, neighbours)
        return out.reshape(-1)

    rows = P(("dom", "sub"), None)
    flat = P(("dom", "sub"))
    return jax.shard_map(
        body, mesh=mesh, in_specs=(flat, rows, rows, rows, rows), out_specs=flat, check_vma=False
    )
```

```python
import functools

import jax
import jax.numpy as jnp
from jax import lax
from jax.experimental import pallas as pl
from jax.experimental.pallas import tpu as pltpu
from jax.sharding import PartitionSpec as P

B = 100
E = 4
LANES = 128
TILES = 25
CHIPS_X = 4
SCALES = (2.0**-44, 1.0, 2.0**44)
SHRINK = 2.0**-12
MESH = pl.DeviceIdType.MESH
F32 = jnp.float32


def lane_of(rows=E):
    return lax.broadcasted_iota(jnp.int32, (rows, LANES), 1)


def periodic(vector):
    lane = lane_of()
    base = jnp.where(lane < B, vector, pltpu.roll(vector, B, 1))
    rolled = {LANES: base}
    for shift in range(4, LANES, 4):
        rolled[shift] = pltpu.roll(base, shift, 1)
    tiles = []
    for j in range(TILES):
        offset = 28 * j % B
        tiles.append(jnp.where(lane < LANES - offset, rolled[LANES - offset], rolled[B - offset]))
    return tiles


def tile_at(ref, j):
    width = min(LANES, ref.shape[1] - j * LANES)
    part = ref[:, j * LANES : j * LANES + width].astype(F32)
    if width < LANES:
        part = jnp.concatenate([part, jnp.zeros((E, LANES - width), F32)], axis=1)
    return part


def row_products(ref, vector):
    lane = lane_of()
    tiles = periodic(vector)
    count = -(-B * B // LANES)
    products = [tile_at(ref, j) * tiles[j % TILES] for j in range(count)]
    sums = []
    for a in range(B):
        j, start = divmod(B * a, LANES)
        if start + B <= LANES:
            row = products[j]
            if start > 0:
                row = jnp.where(lane >= start, row, 0.0)
            if start + B < LANES:
                row = jnp.where(lane < start + B, row, 0.0)
        else:
            row = jnp.where(lane >= start, products[j], jnp.where(lane < start + B - LANES, products[j + 1], 0.0))
        sums.append(jnp.sum(row, axis=1, keepdims=True))
    return sums


def fold(tiles):
    lane = lane_of()
    sums = [None] * 4
    for row in range(TILES * LANES // B):
        j, start = divmod(row * B, LANES)
        part = tiles[j]
        if start + B > LANES:
            part = jnp.where(lane >= start, part, tiles[j + 1])
        if start:
            part = pltpu.roll(part, LANES - start, 1)
        sums[row % 4] = part if sums[row % 4] is None else sums[row % 4] + part
    return jnp.where(lane < B, (sums[0] + sums[1]) + (sums[2] + sums[3]), 0.0)


def column_products(ref, first_row, values):
    lane = lane_of()
    start, stop = first_row * B, (first_row + B) * B
    sums = [None] * TILES
    wide = [jnp.broadcast_to(value, (E, LANES)) for value in values]
    for j in range(start // LANES, -(-stop // LANES)):
        factor = None
        for row in range(j * LANES // B, (j * LANES + LANES - 1) // B + 1):
            begin = row * B - j * LANES
            inside = first_row <= row < first_row + B
            value = wide[row - first_row] if inside else jnp.zeros((E, LANES), F32)
            factor = value if factor is None else jnp.where(lane >= begin, value, factor)
        term = tile_at(ref, j) * factor
        slot = j % TILES
        sums[slot] = term if sums[slot] is None else sums[slot] + term
    return fold(sums)


def unfold(ref, row):
    j, start = divmod(row * B, LANES)
    part = tile_at(ref, j)
    if start + B > LANES:
        part = jnp.where(lane_of() >= start, part, tile_at(ref, j + 1))
    return pltpu.roll(part, LANES - start, 1) if start else part


def weighted(ref, values, rows):
    sums = [None] * 4
    for a, value in enumerate(values):
        term = ref[a] * value[:rows]
        sums[a % 4] = term if sums[a % 4] is None else sums[a % 4] + term
    return jnp.where(lane_of(rows) < B, (sums[0] + sums[1]) + (sums[2] + sums[3]), 0.0)


def as_rows(values):
    lane = lane_of()
    out = jnp.zeros((E, LANES), F32)
    for a, value in enumerate(values):
        out = jnp.where(lane == a, value[:E], out)
    return out


def kernel(
    sizes, rhs_hbm, diag_hbm, face_hbm, prec_hbm, near_hbm, out_ref,
    rhs_ref, diag_ref, face_ref, prec_ref, near_ref, prec_rows, diag_rows, outer_rows, inner_rows, load_sem,
    inner_out, outer_out, inner_one, outer_one, inner_two, outer_two, rhs_box, own_box, own_out, sum_box, sum_out,
    sems, known_a, known_b, known_c, known_d,
):
    doms, subs = sizes
    chips_z = doms // CHIPS_X
    d, s = lax.axis_index("dom"), lax.axis_index("sub")
    x, z = d // chips_z, d % chips_z
    slab = subs * E

    loads = [
        pltpu.make_async_copy(src, dst, load_sem.at[i])
        for i, (src, dst) in enumerate(
            [
                (rhs_hbm, rhs_ref), (prec_hbm, prec_ref), (face_hbm, face_ref), (near_hbm, near_ref),
                (diag_hbm, diag_ref),
            ]
        )
    ]
    mates = [(s + k) % subs for k in range(subs)]
    rows_x = [(x + k) % CHIPS_X * chips_z for k in range(CHIPS_X)]
    rows_z = [(z + k) % chips_z for k in range(chips_z)]
    far_first = sorted(range(1, subs), key=lambda k: -min(k // 2, subs // 2 - k // 2))
    above, below = (d + 1) % doms, (d + doms - 1) % doms

    def along_z(step):
        return rows_x[0] + rows_z[step % chips_z], s

    def along_x(step):
        return rows_x[step % CHIPS_X] + z, s

    barrier = pltpu.get_barrier_semaphore()

    def tell(semaphore, devices):
        for device in devices:
            pl.semaphore_signal(semaphore, inc=1, device_id=device, device_id_type=MESH)

    beside = [(above, s), (below, s), along_z(1), along_z(-1), along_x(1), along_x(-1)]
    tell(barrier, [(d, mates[k]) for k in far_first])
    for load in loads:
        load.start()
    tell(barrier, beside)

    def tell_a():
        tell(known_a, beside)

    def tell_b():
        pl.semaphore_wait(known_a, len(beside))
        tell(known_b, [along_z(2), along_z(-2), along_z(1), along_z(-1)])

    def tell_c():
        pl.semaphore_wait(known_b, 4)
        tell(known_c, [along_z(4), along_z(-4)])

    def tell_d():
        pl.semaphore_wait(known_c, 2)
        tell(known_d, [along_z(2), along_z(-2)])

    def send(src, dst, device, group):
        pltpu.make_async_remote_copy(
            src_ref=src,
            dst_ref=dst,
            send_sem=sems.at[group, 0],
            recv_sem=sems.at[group, 1],
            device_id=device,
            device_id_type=MESH,
        ).start()

    filled = [
        inner_one, outer_one, inner_two, outer_two, rhs_box.at[pl.ds(0, subs - 1)], own_box.at[pl.ds(0, subs - 1)],
        sum_box.at[pl.ds(1, doms - 1)],
    ]
    INNER_ONE, OUTER_ONE, INNER_TWO, OUTER_TWO, RHS, OWN, SUM = range(7)

    def arrived(*groups):
        for group in groups:
            pltpu.make_async_copy(filled[group], filled[group], sems.at[group, 1]).wait()

    goal = {}

    def placed(rows, faces, sent):
        row = lax.broadcasted_iota(jnp.int32, (rows, LANES), 0)
        out = jnp.zeros((rows, LANES), F32)
        for i, face in enumerate(faces):
            for e in range(E):
                out = out + jnp.where(row == goal[e, face], sent[E * i + e : E * i + e + 1], 0.0)
        return out

    def pair_products(faces, values):
        return jnp.concatenate([column_products(face_ref, face * B, values) for face in faces], axis=0)

    def store_slab(ref, value):
        for k in range(subs):
            ref[k] = value[E * k : E * k + E]

    loads[0].wait()
    flat = jnp.concatenate([rhs_ref[...] * SHRINK, jnp.zeros((1, E * LANES - E * B), F32)], axis=1)
    start = jnp.concatenate([flat[:, B * e : B * e + B] for e in range(E)], axis=0)
    start = jnp.concatenate([start, jnp.zeros((E, LANES - B), F32)], axis=1)
    rhs_box[s] = start

    loads[1].wait()
    values = row_products(prec_ref, start)
    loads[2].wait()
    loads[3].wait()
    for e in range(E):
        for face in range(4):
            near = near_ref[e, face]
            row = near - d * slab if face >= 2 else near % E + (E if face == 0 else 0)
            goal[e, face] = jnp.where(near >= 0, row, -1)
    store_slab(inner_out.at[0], placed(slab, (2, 3), pair_products((2, 3), values)))
    pl.semaphore_wait(barrier, subs - 1 + len(beside))
    for k in far_first:
        send(inner_out.at[0, mates[k]], inner_one.at[k - 1], (d, mates[k]), INNER_ONE)
    outer = placed(2 * E, (0, 1), pair_products((0, 1), values))
    outer_out[0, 0] = outer[:E]
    outer_out[0, 1] = outer[E:]
    send(outer_out.at[0, 0], outer_one.at[0], (above, s), OUTER_ONE)
    send(outer_out.at[0, 1], outer_one.at[1], (below, s), OUTER_ONE)
    tell_a()
    for k in far_first:
        send(rhs_box.at[s], rhs_box.at[s], (d, mates[k]), RHS)
    loads[4].wait()
    image = inner_out[0, s] + column_products(diag_ref, 0, values)
    search_one = as_rows(values)

    for a in range(B):
        row = unfold(prec_ref, a)
        prec_rows[a] = jnp.concatenate([row, row], axis=0)
        diag_rows[a] = unfold(diag_ref, a)
        outer_rows[a] = jnp.concatenate([unfold(face_ref, a), unfold(face_ref, B + a)], axis=0)
        inner_rows[a] = jnp.concatenate([unfold(face_ref, 2 * B + a), unfold(face_ref, 3 * B + a)], axis=0)
    tell_b()
    tell_c()
    arrived(INNER_ONE, OUTER_ONE)
    for k in range(subs - 1):
        image = image + inner_one[k]
    image = image + outer_one[0] + outer_one[1]

    twice = jnp.concatenate([image, image], axis=0)
    values = [jnp.sum(prec_rows[a] * twice, axis=1, keepdims=True) for a in range(B)]
    outer = placed(2 * E, (0, 1), weighted(outer_rows, values, 2 * E))
    outer_out[1, 0] = outer[:E]
    outer_out[1, 1] = outer[E:]
    for k in far_first + [0]:
        send(outer_out.at[1, 0], outer_two.at[0, s], (above, mates[k]), OUTER_TWO)
        send(outer_out.at[1, 1], outer_two.at[1, s], (below, mates[k]), OUTER_TWO)
    store_slab(inner_out.at[1], placed(slab, (2, 3), weighted(inner_rows, values, 2 * E)))
    for k in far_first:
        send(inner_out.at[1], inner_two.at[k - 1], (d, mates[k]), INNER_TWO)
    own_out[0] = image
    own_out[1] = weighted(diag_rows, values, E)
    for k in far_first:
        send(own_out, own_box.at[s], (d, mates[k]), OWN)
    own_box[s] = own_out[...]
    search_two = as_rows(values)
    flat_one, flat_two = (
        jnp.concatenate([rows[e : e + 1, :B] * (1.0 / SHRINK) for e in range(E)], axis=1)
        for rows in (search_one, search_two)
    )
    tell_d()
    arrived(RHS, OUTER_TWO, INNER_TWO, OWN)

    products = []
    for k in range(subs):
        rhs, one = rhs_box[k], own_box[k, 0]
        two = own_box[k, 1] + outer_two[0, k] + outer_two[1, k] + inner_out[1, k]
        for m in range(subs - 1):
            two = two + inner_two[m, k]
        terms = [one * rhs, two * rhs]
        for scale in SCALES:
            low_one, low_two = one * scale, two * (scale * scale)
            terms += [low_one * low_one, low_one * low_two, low_two * low_two]
        products = [a + b for a, b in zip(products, terms)] if products else terms
    lane = lane_of(1)
    row = lax.broadcasted_iota(jnp.int32, (16, LANES), 0)
    table = jnp.zeros((16, LANES), F32)
    for q, product in enumerate(products):
        table = jnp.where(row == q, jnp.sum(product, axis=0, keepdims=True), table)
    table = jnp.where(row == lane_of(16), jnp.sum(table, axis=1, keepdims=True), 0.0)
    message = jnp.sum(table, axis=0, keepdims=True)

    pl.semaphore_wait(known_d, 2)
    sum_out[...] = message
    sum_box[0:1] = message
    for k_z in sorted(range(chips_z), key=lambda k: -min(k, chips_z - k)):
        for k_x in sorted(range(CHIPS_X), key=lambda k: -min(k, CHIPS_X - k)):
            k = k_x * chips_z + k_z
            if k:
                send(sum_out, sum_box.at[pl.ds(k, 1)], (rows_x[k_x] + rows_z[k_z], s), SUM)
    arrived(SUM)
    message = jnp.sum(sum_box[...], axis=0, keepdims=True)

    def entry(q):
        return jnp.sum(jnp.where(lane == q, message, 0.0), axis=1, keepdims=True)

    def pick(q):
        low, mid, high = (entry(2 + 3 * i + q) for i in range(3))
        return jnp.where(too_large, low, jnp.where(too_small, high, mid))

    size = entry(2 + 3 + 2)
    too_large = jnp.logical_not(size < 1e26)
    too_small = size < 1e-26
    scale = jnp.where(too_large, SCALES[0], jnp.where(too_small, SCALES[2], SCALES[1]))
    one_one, one_two, two_two = pick(0), pick(1), pick(2)
    one_rhs, two_rhs = entry(0) * scale, entry(1) * scale * scale
    slope = one_two / one_one
    rest = jnp.maximum(two_two - slope * one_two, two_two * 2.0**-22)
    second = (two_rhs - slope * one_rhs) / rest
    first = one_rhs / one_one - slope * second
    out_ref[...] = first * scale * flat_one + second * scale * scale * flat_two

    for group, ref in enumerate(filled):
        pltpu.make_async_copy(ref, ref, sems.at[group, 0]).wait()


def solution(mesh):
    doms, subs = mesh.shape["dom"], mesh.shape["sub"]

    def body(rhs, diag, faces, precond, neighbours):
        out = pl.pallas_call(
            functools.partial(kernel, (doms, subs)),
            out_shape=pltpu.VMEM((1, E * B), F32),
            in_specs=[pl.BlockSpec(memory_space=pltpu.HBM)] * 5,
            out_specs=pl.BlockSpec(memory_space=pltpu.VMEM),
            scratch_shapes=[
                pltpu.VMEM((1, E * B), F32),
                pltpu.VMEM(diag.shape, diag.dtype),
                pltpu.VMEM(faces.shape, faces.dtype),
                pltpu.VMEM(precond.shape, precond.dtype),
                pltpu.SMEM(neighbours.shape, neighbours.dtype),
                pltpu.VMEM((B, 2 * E, LANES), F32),
                pltpu.VMEM((B, E, LANES), F32),
                pltpu.VMEM((B, 2 * E, LANES), F32),
                pltpu.VMEM((B, 2 * E, LANES), F32),
                pltpu.SemaphoreType.DMA((5,)),
                pltpu.VMEM((2, subs, E, LANES), F32),
                pltpu.VMEM((2, 2, E, LANES), F32),
                pltpu.VMEM((subs - 1, E, LANES), F32),
                pltpu.VMEM((2, E, LANES), F32),
                pltpu.VMEM((subs - 1, subs, E, LANES), F32),
                pltpu.VMEM((2, subs, E, LANES), F32),
                pltpu.VMEM((subs, E, LANES), F32),
                pltpu.VMEM((subs, 2, E, LANES), F32),
                pltpu.VMEM((2, E, LANES), F32),
                pltpu.VMEM((doms, LANES), F32),
                pltpu.VMEM((1, LANES), F32),
                pltpu.SemaphoreType.DMA((7, 2)),
                pltpu.SemaphoreType.REGULAR,
                pltpu.SemaphoreType.REGULAR,
                pltpu.SemaphoreType.REGULAR,
                pltpu.SemaphoreType.REGULAR,
            ],
            compiler_params=pltpu.CompilerParams(
                collective_id=0, has_side_effects=True, vmem_limit_bytes=62 * 2**20
            ),
            cost_estimate=pl.CostEstimate(flops=2_000_000, bytes_accessed=500_000, transcendentals=0),
        )(rhs.reshape(1, -1), diag, faces, precond, neighbours)
        return out.reshape(-1)

    rows = P(("dom", "sub"), None)
    flat = P(("dom", "sub"))
    return jax.shard_map(
        body, mesh=mesh, in_specs=(flat, rows, rows, rows, rows), out_specs=flat, check_vma=False
    )
```

```python
import functools

import jax
import jax.numpy as jnp
from jax import lax
from jax.experimental import pallas as pl
from jax.experimental.pallas import tpu as pltpu
from jax.sharding import PartitionSpec as P

B = 100
E = 4
LANES = 128
TILES = 25
CHIPS_X = 4
SCALES = (2.0**-44, 1.0, 2.0**44)
SHRINK = 2.0**-12
MESH = pl.DeviceIdType.MESH
F32 = jnp.float32


def lane_of(rows=E):
    return lax.broadcasted_iota(jnp.int32, (rows, LANES), 1)


def periodic(vector):
    lane = lane_of()
    base = jnp.where(lane < B, vector, pltpu.roll(vector, B, 1))
    rolled = {LANES: base}
    for shift in range(4, LANES, 4):
        rolled[shift] = pltpu.roll(base, shift, 1)
    tiles = []
    for j in range(TILES):
        offset = 28 * j % B
        tiles.append(jnp.where(lane < LANES - offset, rolled[LANES - offset], rolled[B - offset]))
    return tiles


def tile_at(ref, j):
    width = min(LANES, ref.shape[1] - j * LANES)
    part = ref[:, j * LANES : j * LANES + width].astype(F32)
    if width < LANES:
        part = jnp.concatenate([part, jnp.zeros((E, LANES - width), F32)], axis=1)
    return part


def row_products(ref, vector):
    lane = lane_of()
    tiles = periodic(vector)
    count = -(-B * B // LANES)
    products = [tile_at(ref, j) * tiles[j % TILES] for j in range(count)]
    sums = []
    for a in range(B):
        j, start = divmod(B * a, LANES)
        if start + B <= LANES:
            row = products[j]
            if start > 0:
                row = jnp.where(lane >= start, row, 0.0)
            if start + B < LANES:
                row = jnp.where(lane < start + B, row, 0.0)
        else:
            row = jnp.where(lane >= start, products[j], jnp.where(lane < start + B - LANES, products[j + 1], 0.0))
        sums.append(jnp.sum(row, axis=1, keepdims=True))
    return sums


def fold(tiles):
    lane = lane_of()
    sums = [None] * 4
    for row in range(TILES * LANES // B):
        j, start = divmod(row * B, LANES)
        part = tiles[j]
        if start + B > LANES:
            part = jnp.where(lane >= start, part, tiles[j + 1])
        if start:
            part = pltpu.roll(part, LANES - start, 1)
        sums[row % 4] = part if sums[row % 4] is None else sums[row % 4] + part
    return jnp.where(lane < B, (sums[0] + sums[1]) + (sums[2] + sums[3]), 0.0)


def column_products(ref, first_row, values):
    lane = lane_of()
    start, stop = first_row * B, (first_row + B) * B
    sums = [None] * TILES
    wide = [jnp.broadcast_to(value, (E, LANES)) for value in values]
    for j in range(start // LANES, -(-stop // LANES)):
        factor = None
        for row in range(j * LANES // B, (j * LANES + LANES - 1) // B + 1):
            begin = row * B - j * LANES
            inside = first_row <= row < first_row + B
            value = wide[row - first_row] if inside else jnp.zeros((E, LANES), F32)
            factor = value if factor is None else jnp.where(lane >= begin, value, factor)
        term = tile_at(ref, j) * factor
        slot = j % TILES
        sums[slot] = term if sums[slot] is None else sums[slot] + term
    return fold(sums)


def unfold(ref, row):
    j, start = divmod(row * B, LANES)
    part = tile_at(ref, j)
    if start + B > LANES:
        part = jnp.where(lane_of() >= start, part, tile_at(ref, j + 1))
    return pltpu.roll(part, LANES - start, 1) if start else part


def weighted(ref, values, rows):
    sums = [None] * 4
    for a, value in enumerate(values):
        term = ref[a] * value[:rows]
        sums[a % 4] = term if sums[a % 4] is None else sums[a % 4] + term
    return jnp.where(lane_of(rows) < B, (sums[0] + sums[1]) + (sums[2] + sums[3]), 0.0)


def as_rows(values):
    lane = lane_of()
    out = jnp.zeros((E, LANES), F32)
    for a, value in enumerate(values):
        out = jnp.where(lane == a, value[:E], out)
    return out


def kernel(
    sizes, rhs_hbm, diag_hbm, face_hbm, prec_hbm, near_hbm, out_ref,
    rhs_ref, diag_ref, face_ref, prec_ref, near_ref, prec_rows, diag_rows, outer_rows, inner_rows, load_sem,
    inner_out, outer_out, inner_one, outer_one, inner_two, outer_two, rhs_box, own_box, sum_box, sum_out,
    sems, known_a, known_b, known_c, known_d,
):
    doms, subs = sizes
    chips_z = doms // CHIPS_X
    d, s = lax.axis_index("dom"), lax.axis_index("sub")
    x, z = d // chips_z, d % chips_z
    slab = subs * E

    split = 2 * B * B // LANES * LANES
    early, late = pl.ds(0, split), pl.ds(split, 4 * B * B - split)
    loads = [
        pltpu.make_async_copy(src, dst, load_sem.at[i])
        for i, (src, dst) in enumerate(
            [
                (rhs_hbm, rhs_ref), (prec_hbm, prec_ref), (face_hbm.at[:, late], face_ref.at[:, late]), (near_hbm, near_ref),
                (diag_hbm, diag_ref), (face_hbm.at[:, early], face_ref.at[:, early]),
            ]
        )
    ]
    mates = [(s + k) % subs for k in range(subs)]
    rows_x = [(x + k) % CHIPS_X * chips_z for k in range(CHIPS_X)]
    rows_z = [(z + k) % chips_z for k in range(chips_z)]
    far_first = sorted(range(1, subs), key=lambda k: -min(k // 2, subs // 2 - k // 2))
    above, below = (d + 1) % doms, (d + doms - 1) % doms

    def along_z(step):
        return rows_x[0] + rows_z[step % chips_z], s

    def along_x(step):
        return rows_x[step % CHIPS_X] + z, s

    barrier = pltpu.get_barrier_semaphore()

    def tell(semaphore, devices):
        for device in devices:
            pl.semaphore_signal(semaphore, inc=1, device_id=device, device_id_type=MESH)

    beside = [(above, s), (below, s), along_z(1), along_z(-1), along_x(1), along_x(-1)]
    tell(barrier, [(d, mates[k]) for k in far_first])
    for load in loads:
        load.start()
    tell(barrier, beside)

    def tell_a():
        tell(known_a, beside)

    def tell_b():
        pl.semaphore_wait(known_a, len(beside))
        tell(known_b, [along_z(2), along_z(-2), along_z(1), along_z(-1)])

    def tell_c():
        pl.semaphore_wait(known_b, 4)
        tell(known_c, [along_z(4), along_z(-4)])

    def tell_d():
        pl.semaphore_wait(known_c, 2)
        tell(known_d, [along_z(2), along_z(-2)])

    def send(src, dst, device, group):
        pltpu.make_async_remote_copy(
            src_ref=src,
            dst_ref=dst,
            send_sem=sems.at[group, 0],
            recv_sem=sems.at[group, 1],
            device_id=device,
            device_id_type=MESH,
        ).start()

    filled = [
        inner_one, outer_one, inner_two, outer_two, rhs_box.at[pl.ds(0, subs - 1)], own_box.at[pl.ds(0, subs - 1)],
        sum_box.at[pl.ds(1, doms - 1)],
    ]
    INNER_ONE, OUTER_ONE, INNER_TWO, OUTER_TWO, RHS, OWN, SUM = range(7)

    def arrived(*groups):
        for group in groups:
            pltpu.make_async_copy(filled[group], filled[group], sems.at[group, 1]).wait()

    goal = {}

    def placed(rows, faces, sent):
        row = lax.broadcasted_iota(jnp.int32, (rows, LANES), 0)
        out = jnp.zeros((rows, LANES), F32)
        for i, face in enumerate(faces):
            for e in range(E):
                out = out + jnp.where(row == goal[e, face], sent[E * i + e : E * i + e + 1], 0.0)
        return out

    def pair_products(faces, values):
        return jnp.concatenate([column_products(face_ref, face * B, values) for face in faces], axis=0)

    def store_slab(ref, value):
        for k in range(subs):
            ref[k] = value[E * k : E * k + E]

    loads[0].wait()
    flat = jnp.concatenate([rhs_ref[...] * SHRINK, jnp.zeros((1, E * LANES - E * B), F32)], axis=1)
    start = jnp.concatenate([flat[:, B * e : B * e + B] for e in range(E)], axis=0)
    start = jnp.concatenate([start, jnp.zeros((E, LANES - B), F32)], axis=1)
    rhs_box[s] = start

    loads[1].wait()
    values = row_products(prec_ref, start)
    loads[2].wait()
    loads[3].wait()
    for e in range(E):
        for face in range(4):
            near = near_ref[e, face]
            row = near - d * slab if face >= 2 else near % E + (E if face == 0 else 0)
            goal[e, face] = jnp.where(near >= 0, row, -1)
    store_slab(inner_out.at[0], placed(slab, (2, 3), pair_products((2, 3), values)))
    pl.semaphore_wait(barrier, subs - 1 + len(beside))
    for k in far_first:
        send(inner_out.at[0, mates[k]], inner_one.at[k - 1], (d, mates[k]), INNER_ONE)
    loads[5].wait()
    outer = placed(2 * E, (0, 1), pair_products((0, 1), values))
    outer_out[0, 0] = outer[:E]
    outer_out[0, 1] = outer[E:]
    send(outer_out.at[0, 0], outer_one.at[0], (above, s), OUTER_ONE)
    send(outer_out.at[0, 1], outer_one.at[1], (below, s), OUTER_ONE)
    tell_a()
    for k in far_first:
        send(rhs_box.at[s], rhs_box.at[s], (d, mates[k]), RHS)
    loads[4].wait()
    image = inner_out[0, s] + column_products(diag_ref, 0, values)
    search_one = as_rows(values)

    for a in range(B):
        row = unfold(prec_ref, a)
        prec_rows[a] = jnp.concatenate([row, row], axis=0)
        diag_rows[a] = unfold(diag_ref, a)
        outer_rows[a] = jnp.concatenate([unfold(face_ref, a), unfold(face_ref, B + a)], axis=0)
        inner_rows[a] = jnp.concatenate([unfold(face_ref, 2 * B + a), unfold(face_ref, 3 * B + a)], axis=0)
    tell_b()
    tell_c()
    arrived(INNER_ONE, OUTER_ONE)
    for k in range(subs - 1):
        image = image + inner_one[k]
    image = image + outer_one[0] + outer_one[1]

    twice = jnp.concatenate([image, image], axis=0)
    values = [jnp.sum(prec_rows[a] * twice, axis=1, keepdims=True) for a in range(B)]
    outer = placed(2 * E, (0, 1), weighted(outer_rows, values, 2 * E))
    outer_out[1, 0] = outer[:E]
    outer_out[1, 1] = outer[E:]
    for k in far_first + [0]:
        send(outer_out.at[1, 0], outer_two.at[0, s], (above, mates[k]), OUTER_TWO)
        send(outer_out.at[1, 1], outer_two.at[1, s], (below, mates[k]), OUTER_TWO)
    own_box[s] = image
    for k in far_first:
        send(own_box.at[s], own_box.at[s], (d, mates[k]), OWN)
    own = weighted(diag_rows, values, E)
    store_slab(inner_out.at[1], placed(slab, (2, 3), weighted(inner_rows, values, 2 * E)))
    inner_out[1, s] = inner_out[1, s] + own
    for k in far_first:
        send(inner_out.at[1], inner_two.at[k - 1], (d, mates[k]), INNER_TWO)
    search_two = as_rows(values)
    flat_one, flat_two = (
        jnp.concatenate([rows[e : e + 1, :B] * (1.0 / SHRINK) for e in range(E)], axis=1)
        for rows in (search_one, search_two)
    )
    tell_d()

    def over_slab(terms):
        return functools.reduce(lambda a, b: [p + q for p, q in zip(a, b)], [terms(k) for k in range(subs)])

    def early_terms(k):
        one = own_box[k]
        return [one * rhs_box[k]] + [(one * scale) * (one * scale) for scale in SCALES]

    def late_terms(k):
        two = (outer_two[0, k] + outer_two[1, k]) + inner_out[1, k]
        for m in range(subs - 1):
            two = two + inner_two[m, k]
        terms = [two * rhs_box[k]]
        for scale in SCALES:
            low_one, low_two = own_box[k] * scale, two * (scale * scale)
            terms += [low_one * low_two, low_two * low_two]
        return terms

    arrived(RHS, OWN)
    early = over_slab(early_terms)
    arrived(OUTER_TWO, INNER_TWO)
    late = over_slab(late_terms)
    products = [early[0], late[0]]
    for i in range(len(SCALES)):
        products += [early[1 + i], late[1 + 2 * i], late[2 + 2 * i]]
    lane = lane_of(1)
    row = lax.broadcasted_iota(jnp.int32, (16, LANES), 0)
    table = jnp.zeros((16, LANES), F32)
    for q, product in enumerate(products):
        table = jnp.where(row == q, jnp.sum(product, axis=0, keepdims=True), table)
    table = jnp.where(row == lane_of(16), jnp.sum(table, axis=1, keepdims=True), 0.0)
    message = jnp.sum(table, axis=0, keepdims=True)

    pl.semaphore_wait(known_d, 2)
    sum_out[...] = message
    sum_box[0:1] = message
    for k_z in sorted(range(chips_z), key=lambda k: -min(k, chips_z - k)):
        for k_x in sorted(range(CHIPS_X), key=lambda k: -min(k, CHIPS_X - k)):
            k = k_x * chips_z + k_z
            if k:
                send(sum_out, sum_box.at[pl.ds(k, 1)], (rows_x[k_x] + rows_z[k_z], s), SUM)
    arrived(SUM)
    message = jnp.sum(sum_box[...], axis=0, keepdims=True)

    def entry(q):
        return jnp.sum(jnp.where(lane == q, message, 0.0), axis=1, keepdims=True)

    def pick(q):
        low, mid, high = (entry(2 + 3 * i + q) for i in range(3))
        return jnp.where(too_large, low, jnp.where(too_small, high, mid))

    size = entry(2 + 3 + 2)
    too_large = jnp.logical_not(size < 1e26)
    too_small = size < 1e-26
    scale = jnp.where(too_large, SCALES[0], jnp.where(too_small, SCALES[2], SCALES[1]))
    one_one, one_two, two_two = pick(0), pick(1), pick(2)
    one_rhs, two_rhs = entry(0) * scale, entry(1) * scale * scale
    slope = one_two / one_one
    rest = jnp.maximum(two_two - slope * one_two, two_two * 2.0**-22)
    second = (two_rhs - slope * one_rhs) / rest
    first = one_rhs / one_one - slope * second
    out_ref[...] = first * scale * flat_one + second * scale * scale * flat_two

    for group, ref in enumerate(filled):
        pltpu.make_async_copy(ref, ref, sems.at[group, 0]).wait()


def solution(mesh):
    doms, subs = mesh.shape["dom"], mesh.shape["sub"]

    def body(rhs, diag, faces, precond, neighbours):
        out = pl.pallas_call(
            functools.partial(kernel, (doms, subs)),
            out_shape=pltpu.VMEM((1, E * B), F32),
            in_specs=[pl.BlockSpec(memory_space=pltpu.HBM)] * 5,
            out_specs=pl.BlockSpec(memory_space=pltpu.VMEM),
            scratch_shapes=[
                pltpu.VMEM((1, E * B), F32),
                pltpu.VMEM(diag.shape, diag.dtype),
                pltpu.VMEM(faces.shape, faces.dtype),
                pltpu.VMEM(precond.shape, precond.dtype),
                pltpu.SMEM(neighbours.shape, neighbours.dtype),
                pltpu.VMEM((B, 2 * E, LANES), F32),
                pltpu.VMEM((B, E, LANES), F32),
                pltpu.VMEM((B, 2 * E, LANES), F32),
                pltpu.VMEM((B, 2 * E, LANES), F32),
                pltpu.SemaphoreType.DMA((6,)),
                pltpu.VMEM((2, subs, E, LANES), F32),
                pltpu.VMEM((2, 2, E, LANES), F32),
                pltpu.VMEM((subs - 1, E, LANES), F32),
                pltpu.VMEM((2, E, LANES), F32),
                pltpu.VMEM((subs - 1, subs, E, LANES), F32),
                pltpu.VMEM((2, subs, E, LANES), F32),
                pltpu.VMEM((subs, E, LANES), F32),
                pltpu.VMEM((subs, E, LANES), F32),
                pltpu.VMEM((doms, LANES), F32),
                pltpu.VMEM((1, LANES), F32),
                pltpu.SemaphoreType.DMA((7, 2)),
                pltpu.SemaphoreType.REGULAR,
                pltpu.SemaphoreType.REGULAR,
                pltpu.SemaphoreType.REGULAR,
                pltpu.SemaphoreType.REGULAR,
            ],
            compiler_params=pltpu.CompilerParams(
                collective_id=0, has_side_effects=True, vmem_limit_bytes=62 * 2**20
            ),
            cost_estimate=pl.CostEstimate(flops=2_000_000, bytes_accessed=500_000, transcendentals=0),
        )(rhs.reshape(1, -1), diag, faces, precond, neighbours)
        return out.reshape(-1)

    rows = P(("dom", "sub"), None)
    flat = P(("dom", "sub"))
    return jax.shard_map(
        body, mesh=mesh, in_specs=(flat, rows, rows, rows, rows), out_specs=flat, check_vma=False
    )
```

```python
import functools

import jax
import jax.numpy as jnp
from jax import lax
from jax.experimental import pallas as pl
from jax.experimental.pallas import tpu as pltpu
from jax.sharding import PartitionSpec as P

B = 100
E = 4
LANES = 128
TILES = 25
CHIPS_X = 4
SCALES = (2.0**-44, 1.0, 2.0**44)
SHRINK = 2.0**-12
MESH = pl.DeviceIdType.MESH
F32 = jnp.float32


def lane_of(rows=E):
    return lax.broadcasted_iota(jnp.int32, (rows, LANES), 1)


def periodic(vector):
    lane = lane_of()
    base = jnp.where(lane < B, vector, pltpu.roll(vector, B, 1))
    rolled = {LANES: base}
    for shift in range(4, LANES, 4):
        rolled[shift] = pltpu.roll(base, shift, 1)
    tiles = []
    for j in range(TILES):
        offset = 28 * j % B
        tiles.append(jnp.where(lane < LANES - offset, rolled[LANES - offset], rolled[B - offset]))
    return tiles


def tile_at(ref, j):
    width = min(LANES, ref.shape[1] - j * LANES)
    part = ref[:, j * LANES : j * LANES + width].astype(F32)
    if width < LANES:
        part = jnp.concatenate([part, jnp.zeros((E, LANES - width), F32)], axis=1)
    return part


def row_products(ref, vector):
    lane = lane_of()
    tiles = periodic(vector)
    count = -(-B * B // LANES)
    products = [tile_at(ref, j) * tiles[j % TILES] for j in range(count)]
    sums = []
    for a in range(B):
        j, start = divmod(B * a, LANES)
        if start + B <= LANES:
            row = products[j]
            if start > 0:
                row = jnp.where(lane >= start, row, 0.0)
            if start + B < LANES:
                row = jnp.where(lane < start + B, row, 0.0)
        else:
            row = jnp.where(lane >= start, products[j], jnp.where(lane < start + B - LANES, products[j + 1], 0.0))
        sums.append(jnp.sum(row, axis=1, keepdims=True))
    return sums


def fold(tiles):
    lane = lane_of()
    sums = [None] * 4
    for row in range(TILES * LANES // B):
        j, start = divmod(row * B, LANES)
        part = tiles[j]
        if start + B > LANES:
            part = jnp.where(lane >= start, part, tiles[j + 1])
        if start:
            part = pltpu.roll(part, LANES - start, 1)
        sums[row % 4] = part if sums[row % 4] is None else sums[row % 4] + part
    return jnp.where(lane < B, (sums[0] + sums[1]) + (sums[2] + sums[3]), 0.0)


def column_products(ref, first_row, values):
    lane = lane_of()
    start, stop = first_row * B, (first_row + B) * B
    sums = [None] * TILES
    wide = [jnp.broadcast_to(value, (E, LANES)) for value in values]
    for j in range(start // LANES, -(-stop // LANES)):
        factor = None
        for row in range(j * LANES // B, (j * LANES + LANES - 1) // B + 1):
            begin = row * B - j * LANES
            inside = first_row <= row < first_row + B
            value = wide[row - first_row] if inside else jnp.zeros((E, LANES), F32)
            factor = value if factor is None else jnp.where(lane >= begin, value, factor)
        term = tile_at(ref, j) * factor
        slot = j % TILES
        sums[slot] = term if sums[slot] is None else sums[slot] + term
    return fold(sums)


def unfold(ref, row):
    j, start = divmod(row * B, LANES)
    part = tile_at(ref, j)
    if start + B > LANES:
        part = jnp.where(lane_of() >= start, part, tile_at(ref, j + 1))
    return pltpu.roll(part, LANES - start, 1) if start else part


def weighted(ref, values, rows):
    sums = [None] * 4
    for a, value in enumerate(values):
        term = ref[a] * value[:rows]
        sums[a % 4] = term if sums[a % 4] is None else sums[a % 4] + term
    return jnp.where(lane_of(rows) < B, (sums[0] + sums[1]) + (sums[2] + sums[3]), 0.0)


def as_rows(values):
    lane = lane_of()
    out = jnp.zeros((E, LANES), F32)
    for a, value in enumerate(values):
        out = jnp.where(lane == a, value[:E], out)
    return out


def kernel(
    sizes, rhs_hbm, diag_hbm, face_hbm, prec_hbm, near_hbm, out_ref,
    rhs_ref, diag_ref, face_ref, prec_ref, near_ref, prec_rows, diag_rows, outer_rows, inner_rows, load_sem,
    inner_out, outer_out, inner_one, outer_one, inner_two, outer_two, rhs_box, own_box, sum_box, sum_out,
    sems, known_a, known_b, known_c, known_d,
):
    doms, subs = sizes
    chips_z = doms // CHIPS_X
    d, s = lax.axis_index("dom"), lax.axis_index("sub")
    x, z = d // chips_z, d % chips_z
    slab = subs * E

    split = 2 * B * B // LANES * LANES
    early, late = pl.ds(0, split), pl.ds(split, 4 * B * B - split)
    loads = [
        pltpu.make_async_copy(src, dst, load_sem.at[i])
        for i, (src, dst) in enumerate(
            [
                (rhs_hbm, rhs_ref), (prec_hbm, prec_ref), (face_hbm.at[:, late], face_ref.at[:, late]), (near_hbm, near_ref),
                (diag_hbm, diag_ref), (face_hbm.at[:, early], face_ref.at[:, early]),
            ]
        )
    ]
    mates = [(s + k) % subs for k in range(subs)]
    rows_x = [(x + k) % CHIPS_X * chips_z for k in range(CHIPS_X)]
    rows_z = [(z + k) % chips_z for k in range(chips_z)]
    far_first = sorted(range(1, subs), key=lambda k: -min(k // 2, subs // 2 - k // 2))
    above, below = (d + 1) % doms, (d + doms - 1) % doms

    def along_z(step):
        return rows_x[0] + rows_z[step % chips_z], s

    def along_x(step):
        return rows_x[step % CHIPS_X] + z, s

    barrier = pltpu.get_barrier_semaphore()

    def tell(semaphore, devices):
        for device in devices:
            pl.semaphore_signal(semaphore, inc=1, device_id=device, device_id_type=MESH)

    beside = [(above, s), (below, s), along_z(1), along_z(-1), along_x(1), along_x(-1)]
    tell(barrier, [(d, mates[k]) for k in far_first])
    for load in loads:
        load.start()
    tell(barrier, beside)

    def tell_a():
        tell(known_a, beside)

    def tell_b():
        pl.semaphore_wait(known_a, len(beside))
        tell(known_b, [along_z(2), along_z(-2), along_z(1), along_z(-1)])

    def tell_c():
        pl.semaphore_wait(known_b, 4)
        tell(known_c, [along_z(4), along_z(-4)])

    def tell_d():
        pl.semaphore_wait(known_c, 2)
        tell(known_d, [along_z(2), along_z(-2)])

    def send(src, dst, device, group):
        pltpu.make_async_remote_copy(
            src_ref=src,
            dst_ref=dst,
            send_sem=sems.at[group, 0],
            recv_sem=sems.at[group, 1],
            device_id=device,
            device_id_type=MESH,
        ).start()

    filled = [
        inner_one, outer_one, inner_two, outer_two, rhs_box.at[pl.ds(0, subs - 1)], own_box.at[pl.ds(0, subs - 1)],
        sum_box.at[pl.ds(1, doms - 1)],
    ]
    INNER_ONE, OUTER_ONE, INNER_TWO, OUTER_TWO, RHS, OWN, SUM = range(7)

    def arrived(*groups):
        for group in groups:
            pltpu.make_async_copy(filled[group], filled[group], sems.at[group, 1]).wait()

    goal = {}

    def placed(rows, faces, sent):
        row = lax.broadcasted_iota(jnp.int32, (rows, LANES), 0)
        out = jnp.zeros((rows, LANES), F32)
        for i, face in enumerate(faces):
            for e in range(E):
                out = out + jnp.where(row == goal[e, face], sent[E * i + e : E * i + e + 1], 0.0)
        return out

    def pair_products(faces, values):
        return jnp.concatenate([column_products(face_ref, face * B, values) for face in faces], axis=0)

    def store_slab(ref, value):
        for k in range(subs):
            ref[k] = value[E * k : E * k + E]

    loads[0].wait()
    flat = jnp.concatenate([rhs_ref[...] * SHRINK, jnp.zeros((1, E * LANES - E * B), F32)], axis=1)
    start = jnp.concatenate([flat[:, B * e : B * e + B] for e in range(E)], axis=0)
    start = jnp.concatenate([start, jnp.zeros((E, LANES - B), F32)], axis=1)
    rhs_box[s] = start

    loads[1].wait()
    values = row_products(prec_ref, start)
    loads[2].wait()
    loads[3].wait()
    for e in range(E):
        for face in range(4):
            near = near_ref[e, face]
            row = near - d * slab if face >= 2 else near % E + (E if face == 0 else 0)
            goal[e, face] = jnp.where(near >= 0, row, -1)
    store_slab(inner_out.at[0], placed(slab, (2, 3), pair_products((2, 3), values)))
    pl.semaphore_wait(barrier, subs - 1 + len(beside))
    for k in far_first:
        send(inner_out.at[0, mates[k]], inner_one.at[k - 1], (d, mates[k]), INNER_ONE)
    loads[5].wait()
    outer = placed(2 * E, (0, 1), pair_products((0, 1), values))
    outer_out[0, 0] = outer[:E]
    outer_out[0, 1] = outer[E:]
    send(outer_out.at[0, 0], outer_one.at[0], (above, s), OUTER_ONE)
    send(outer_out.at[0, 1], outer_one.at[1], (below, s), OUTER_ONE)
    tell_a()
    for k in far_first:
        send(rhs_box.at[s], rhs_box.at[s], (d, mates[k]), RHS)
    loads[4].wait()
    image = inner_out[0, s] + column_products(diag_ref, 0, values)
    search_one = as_rows(values)

    for a in range(B):
        row = unfold(prec_ref, a)
        prec_rows[a] = jnp.concatenate([row, row], axis=0)
        diag_rows[a] = unfold(diag_ref, a)
        outer_rows[a] = jnp.concatenate([unfold(face_ref, a), unfold(face_ref, B + a)], axis=0)
        inner_rows[a] = jnp.concatenate([unfold(face_ref, 2 * B + a), unfold(face_ref, 3 * B + a)], axis=0)
    tell_b()
    tell_c()
    arrived(INNER_ONE, OUTER_ONE)
    for k in range(subs - 1):
        image = image + inner_one[k]
    image = image + outer_one[0] + outer_one[1]

    twice = jnp.concatenate([image, image], axis=0)
    values = [jnp.sum(prec_rows[a] * twice, axis=1, keepdims=True) for a in range(B)]
    outer = placed(2 * E, (0, 1), weighted(outer_rows, values, 2 * E))
    outer_out[1, 0] = outer[:E]
    outer_out[1, 1] = outer[E:]

    def send_outer(places):
        for k in places:
            send(outer_out.at[1, 0], outer_two.at[0, s], (above, mates[k]), OUTER_TWO)
            send(outer_out.at[1, 1], outer_two.at[1, s], (below, mates[k]), OUTER_TWO)

    send_outer(far_first[:2])
    own_box[s] = image
    own = weighted(diag_rows, values, E)
    store_slab(inner_out.at[1], placed(slab, (2, 3), weighted(inner_rows, values, 2 * E)))
    inner_out[1, s] = inner_out[1, s] + own
    for k in far_first:
        send(inner_out.at[1], inner_two.at[k - 1], (d, mates[k]), INNER_TWO)
    send_outer(far_first[2:] + [0])
    for k in far_first:
        send(own_box.at[s], own_box.at[s], (d, mates[k]), OWN)
    search_two = as_rows(values)
    flat_one, flat_two = (
        jnp.concatenate([rows[e : e + 1, :B] * (1.0 / SHRINK) for e in range(E)], axis=1)
        for rows in (search_one, search_two)
    )
    tell_d()

    def over_slab(terms):
        return functools.reduce(lambda a, b: [p + q for p, q in zip(a, b)], [terms(k) for k in range(subs)])

    def early_terms(k):
        one = own_box[k]
        return [one * rhs_box[k]] + [(one * scale) * (one * scale) for scale in SCALES]

    def late_terms(k):
        two = (outer_two[0, k] + outer_two[1, k]) + inner_out[1, k]
        for m in range(subs - 1):
            two = two + inner_two[m, k]
        terms = [two * rhs_box[k]]
        for scale in SCALES:
            low_one, low_two = own_box[k] * scale, two * (scale * scale)
            terms += [low_one * low_two, low_two * low_two]
        return terms

    arrived(RHS, OWN)
    early = over_slab(early_terms)
    arrived(OUTER_TWO, INNER_TWO)
    late = over_slab(late_terms)
    products = [early[0], late[0]]
    for i in range(len(SCALES)):
        products += [early[1 + i], late[1 + 2 * i], late[2 + 2 * i]]
    lane = lane_of(1)
    row = lax.broadcasted_iota(jnp.int32, (16, LANES), 0)
    table = jnp.zeros((16, LANES), F32)
    for q, product in enumerate(products):
        table = jnp.where(row == q, jnp.sum(product, axis=0, keepdims=True), table)
    table = jnp.where(row == lane_of(16), jnp.sum(table, axis=1, keepdims=True), 0.0)
    message = jnp.sum(table, axis=0, keepdims=True)

    pl.semaphore_wait(known_d, 2)
    sum_out[...] = message
    sum_box[0:1] = message
    for k_z in sorted(range(chips_z), key=lambda k: -min(k, chips_z - k)):
        for k_x in sorted(range(CHIPS_X), key=lambda k: -min(k, CHIPS_X - k)):
            k = k_x * chips_z + k_z
            if k:
                send(sum_out, sum_box.at[pl.ds(k, 1)], (rows_x[k_x] + rows_z[k_z], s), SUM)
    arrived(SUM)
    message = jnp.sum(sum_box[...], axis=0, keepdims=True)

    def entry(q):
        return jnp.sum(jnp.where(lane == q, message, 0.0), axis=1, keepdims=True)

    def pick(q):
        low, mid, high = (entry(2 + 3 * i + q) for i in range(3))
        return jnp.where(too_large, low, jnp.where(too_small, high, mid))

    size = entry(2 + 3 + 2)
    too_large = jnp.logical_not(size < 1e26)
    too_small = size < 1e-26
    scale = jnp.where(too_large, SCALES[0], jnp.where(too_small, SCALES[2], SCALES[1]))
    one_one, one_two, two_two = pick(0), pick(1), pick(2)
    one_rhs, two_rhs = entry(0) * scale, entry(1) * scale * scale
    slope = one_two / one_one
    rest = jnp.maximum(two_two - slope * one_two, two_two * 2.0**-22)
    second = (two_rhs - slope * one_rhs) / rest
    first = one_rhs / one_one - slope * second
    out_ref[...] = first * scale * flat_one + second * scale * scale * flat_two

    for group, ref in enumerate(filled):
        pltpu.make_async_copy(ref, ref, sems.at[group, 0]).wait()


def solution(mesh):
    doms, subs = mesh.shape["dom"], mesh.shape["sub"]

    def body(rhs, diag, faces, precond, neighbours):
        out = pl.pallas_call(
            functools.partial(kernel, (doms, subs)),
            out_shape=pltpu.VMEM((1, E * B), F32),
            in_specs=[pl.BlockSpec(memory_space=pltpu.HBM)] * 5,
            out_specs=pl.BlockSpec(memory_space=pltpu.VMEM),
            scratch_shapes=[
                pltpu.VMEM((1, E * B), F32),
                pltpu.VMEM(diag.shape, diag.dtype),
                pltpu.VMEM(faces.shape, faces.dtype),
                pltpu.VMEM(precond.shape, precond.dtype),
                pltpu.SMEM(neighbours.shape, neighbours.dtype),
                pltpu.VMEM((B, 2 * E, LANES), F32),
                pltpu.VMEM((B, E, LANES), F32),
                pltpu.VMEM((B, 2 * E, LANES), F32),
                pltpu.VMEM((B, 2 * E, LANES), F32),
                pltpu.SemaphoreType.DMA((6,)),
                pltpu.VMEM((2, subs, E, LANES), F32),
                pltpu.VMEM((2, 2, E, LANES), F32),
                pltpu.VMEM((subs - 1, E, LANES), F32),
                pltpu.VMEM((2, E, LANES), F32),
                pltpu.VMEM((subs - 1, subs, E, LANES), F32),
                pltpu.VMEM((2, subs, E, LANES), F32),
                pltpu.VMEM((subs, E, LANES), F32),
                pltpu.VMEM((subs, E, LANES), F32),
                pltpu.VMEM((doms, LANES), F32),
                pltpu.VMEM((1, LANES), F32),
                pltpu.SemaphoreType.DMA((7, 2)),
                pltpu.SemaphoreType.REGULAR,
                pltpu.SemaphoreType.REGULAR,
                pltpu.SemaphoreType.REGULAR,
                pltpu.SemaphoreType.REGULAR,
            ],
            compiler_params=pltpu.CompilerParams(
                collective_id=0, has_side_effects=True, vmem_limit_bytes=62 * 2**20
            ),
            cost_estimate=pl.CostEstimate(flops=2_000_000, bytes_accessed=500_000, transcendentals=0),
        )(rhs.reshape(1, -1), diag, faces, precond, neighbours)
        return out.reshape(-1)

    rows = P(("dom", "sub"), None)
    flat = P(("dom", "sub"))
    return jax.shard_map(
        body, mesh=mesh, in_specs=(flat, rows, rows, rows, rows), out_specs=flat, check_vma=False
    )
```
